128 devices in a mesh: dp: 4 (over z), fsdp: 32 (over x, y, core).
Axes of the slice: x: 4, y: 4, z: 4, core: 2. Of those that a mesh axis runs over, the one named last changes fastest.
Arguments:
- grads: bfloat16 [4, 2, 6144, 6144], P('dp', None, 'fsdp'), may hold values from -200 to 200, as said below
- errors: bfloat16 [4, 2, 6144, 6144], P('dp', None, 'fsdp'), may hold values from -3 to 3
- q_init: float32 [2, 6144, 8], replicated, may hold values from -6 to 6
Outputs:
- approx: bfloat16 [2, 6144, 6144], P(None, 'fsdp')
- errors_next: bfloat16 [4, 2, 6144, 6144], P('dp', None, 'fsdp')
- q_next: float32 [2, 6144, 8], replicated
The draws below stay inside these ranges and needn't reach their ends.
Inputs may be any that keep to these rules, and one draw needn't show every extreme that they name: `grads`: gradients of one matrix differ from replica to replica.
All inputs are finite; a program needn't handle non-finite values.
Results may differ from the reference program's by a relative error of at most 0.0027.
Values sent between devices are 32-bit elements; how exact they have to be, the bound alone decides.
No kernel may reach another device: no remote copies, remote signals or barrier semaphores. Data moves between devices by JAX's collectives and lax.ppermute only.
A program may use at most 128 MiB of HBM per device.

```python
import math
import jax
import jax.numpy as jnp
from jax import lax

D = 6144
MATS = 2
RANK = 8
ITERS = 2
N_DP = 4


def draw_grads(key, part):
    key = jax.random.fold_in(key, 11)
    keys = jax.random.split(key, 6)
    left_vec = jnp.clip(jax.random.normal(keys[0], (MATS, 4, D), jnp.float32), -4.0, 4.0)
    right_vec = jnp.clip(jax.random.normal(keys[1], (MATS, 4, D), jnp.float32), -4.0, 4.0)
    strengths = (0.2, 0.15, 0.1, 0.07)
    ramp = 1.0 + 2.0 * jnp.arange(D, dtype=jnp.float32) / (D - 1)
    row_scale = jnp.exp(jax.random.uniform(keys[2], (MATS, D), jnp.float32, math.log(0.5), math.log(2.0))) * ramp[None, :]
    col_scale = jnp.exp(jax.random.uniform(keys[3], (MATS, D), jnp.float32, math.log(0.5), math.log(2.0)))
    replica_gain = jax.random.uniform(keys[4], (N_DP, MATS, 1, 1), jnp.float32, 0.6, 1.4)
    signal = strengths[0] * left_vec[:, 0, :, None] * right_vec[:, 0, None, :]
    signal = signal + strengths[1] * left_vec[:, 1, :, None] * right_vec[:, 1, None, :]
    signal = signal + strengths[2] * left_vec[:, 2, :, None] * right_vec[:, 2, None, :]
    signal = signal + strengths[3] * left_vec[:, 3, :, None] * right_vec[:, 3, None, :]
    noise = jnp.clip(jax.random.normal(keys[5], (N_DP, MATS, D, D), jnp.float32), -4.0, 4.0)
    value = (replica_gain * signal[None] + noise) * row_scale[None, :, :, None] * col_scale[None, :, None, :]
    return value.astype(jnp.bfloat16)


def level_of(stream_key, shape, pieces, least, largest):
    def one(axis_at, shards_of):
        heights = jax.random.uniform(jax.random.fold_in(jax.random.fold_in(stream_key, 6), axis_at), (shards_of,), jnp.float32, least / len(pieces), largest / len(pieces))
        return jnp.repeat(jnp.exp(heights), shape[axis_at] // shards_of).reshape((-1,) + (1,) * (len(shape) - axis_at - 1))

    gain = one(*pieces[0])
    for cut in pieces[1:]:
        gain = gain * one(*cut)
    return gain


def gaussian(rng, extent, spread, reach, cuts=(), kind=jnp.bfloat16):
    loudness = level_of(rng, extent, cuts, -0.22, 0.18) if cuts else 1.0
    result = jax.random.normal(rng, extent, jnp.float32) * spread * loudness
    return jnp.minimum(jnp.maximum(result, -reach), reach).astype(kind)


def setup_inputs(seed: int = 0) -> dict:
    arg_keys = jax.random.split(jax.random.key(seed), 4)
    grads = draw_grads(jax.random.fold_in(arg_keys[3], 71), 0)
    errors = gaussian(arg_keys[1], (N_DP, MATS, D, D), 0.5, 3.0, ((0, 4), (2, 32)))
    q_init = gaussian(arg_keys[2], (MATS, D, RANK), 1.0, 6.0, (), jnp.float32)
    return dict(grads=grads, errors=errors, q_init=q_init)


def orthonormal(p_basis):
    gram = jnp.dot(p_basis.T.astype(jnp.float32), p_basis.astype(jnp.float32), precision=lax.Precision.HIGHEST, preferred_element_type=jnp.float32)
    lower_factor = jnp.linalg.cholesky(gram)
    solved = lax.linalg.triangular_solve(lower_factor, p_basis.T, left_side=True, lower=True)
    return solved.T

def reference(grads, errors, q_init):
    approx_list = []
    error_list = []
    basis_list = []
    for matrix_index in range(MATS):
        working = grads[:, matrix_index].astype(jnp.float32) + errors[:, matrix_index].astype(jnp.float32)
        q_basis = q_init[matrix_index]
        p_hat = None
        for iteration in range(ITERS):
            p_basis = jnp.sum(jnp.einsum('rij,jk->rik', working, q_basis, precision=lax.Precision.HIGHEST), axis=0) / N_DP
            p_hat = orthonormal(p_basis)
            q_basis = jnp.sum(jnp.einsum('rij,ik->rjk', working, p_hat, precision=lax.Precision.HIGHEST), axis=0) / N_DP
        full = jnp.dot(p_hat.astype(jnp.float32), q_basis.T.astype(jnp.float32), precision=lax.Precision.HIGHEST, preferred_element_type=jnp.float32)
        approx_list.append(full.astype(jnp.bfloat16))
        error_list.append((working - full[None]).astype(jnp.bfloat16))
        basis_list.append(q_basis)
    return (jnp.stack(approx_list, 0), jnp.stack(error_list, 1), jnp.stack(basis_list, 0))
```

```python
import functools

import jax
import jax.numpy as jnp
from jax import lax
from jax.experimental import pallas as pl
from jax.experimental.pallas import tpu as pltpu
from jax.sharding import Mesh, PartitionSpec as P

F32, BF16 = jnp.float32, jnp.bfloat16
MATS, RANK, ROWS, COLS = 2, 8, 192, 6144
CHUNK = 1024
STEPS = COLS // CHUNK
TILES = CHUNK // 128
GRAM = MATS * COLS // 128
N_DEV, N_DP = 128, 4
VMEM = 48 * 1024 * 1024
ALL = ("dp", "x", "y", "core")


def split3(a):
    one = a.astype(BF16).astype(F32)
    rest = a - one
    two = rest.astype(BF16).astype(F32)
    return one, two, rest - two


def three(a):
    return jnp.concatenate(split3(a), axis=0).astype(BF16)


def fold(r):
    return r[0:8] + r[8:16] + r[16:24]


def small_dot(a, b):
    total = a[:, 0:1] * b[0:1, :]
    for k in range(1, RANK):
        total = total + a[:, k : k + 1] * b[k : k + 1, :]
    return total


def inverse_lower(gram):
    row = lax.broadcasted_iota(jnp.int32, (8, 128), 0)
    lane = lax.broadcasted_iota(jnp.int32, (8, 128), 1)
    a = jnp.where(lane < RANK, gram, jnp.where(lane == row + RANK, 1.0, 0.0).astype(F32))
    for k in range(RANK):
        pivot = a[k : k + 1, k : k + 1]
        inv = lax.rsqrt(pivot)
        inv = inv * (1.5 - 0.5 * pivot * inv * inv)
        top = a[k : k + 1, :] * inv
        below = a - (a[:, k : k + 1] * inv) * top
        a = jnp.where(row == k, top, jnp.where(row > k, below, a))
    return a[:, RANK : 2 * RANK]


def left_kernel(tiled, g_ref, e_ref, q_ref, *refs):
    if tiled:
        gram_ref, o_ref, acc = refs
    else:
        o_ref, acc = refs
    j = pl.program_id(0)

    @pl.when(j == 0)
    def _():
        acc[...] = jnp.zeros_like(acc)

    for m in range(MATS):
        if tiled:
            q = jnp.concatenate([q_ref[m * TILES + c] for c in range(TILES)], axis=1)
        else:
            q = q_ref[m]
        q = three(q)
        dims = (((1,), (1,)), ((), ()))
        r = lax.dot_general(q, g_ref[0, m], dims, preferred_element_type=F32)
        r = r + lax.dot_general(q, e_ref[0, m], dims, preferred_element_type=F32)
        acc[m] += r

    @pl.when(j == STEPS - 1)
    def _():
        for m in range(MATS):
            p = fold(acc[m])
            if tiled:
                lower_inv = inverse_lower(gram_ref[m])
                p = small_dot(lower_inv, p)
            o_ref[m * 8 : (m + 1) * 8, :] = p


def left(g, e, q, gram_from=None):
    tiled = gram_from is not None
    w_spec = pl.BlockSpec((1, MATS, ROWS, CHUNK), lambda j: (0, 0, 0, j))
    if tiled:
        specs = [w_spec, w_spec, pl.BlockSpec((MATS * TILES, 8, 128), lambda j: (j, 0, 0)),
                 pl.BlockSpec((MATS, 8, 128), lambda j: (GRAM // MATS, 0, 0))]
        args = (g, e, q, gram_from)
    else:
        specs = [w_spec, w_spec, pl.BlockSpec((MATS, RANK, CHUNK), lambda j: (0, 0, j))]
        args = (g, e, q)
    return pl.pallas_call(
        functools.partial(left_kernel, tiled),
        grid=(STEPS,),
        in_specs=specs,
        out_specs=pl.BlockSpec((16, ROWS), lambda j: (0, 0)),
        out_shape=jax.ShapeDtypeStruct((16, ROWS), F32),
        scratch_shapes=[pltpu.VMEM((MATS, 24, ROWS), F32)],
        compiler_params=pltpu.CompilerParams(vmem_limit_bytes=VMEM),
        name="left_factor",
    )(*args)


def right_kernel(p_ref, g_ref, e_ref, o_ref, psum_ref, p3):
    j = pl.program_id(0)

    @pl.when(j == 0)
    def _():
        p = (p_ref[0] + p_ref[1] + p_ref[2] + p_ref[3]) * (1.0 / N_DP)
        psum_ref[...] = p
        for m in range(MATS):
            p3[m] = three(p[m * 8 : (m + 1) * 8])

    @pl.when(j < STEPS)
    def _():
        for m in range(MATS):
            r = jnp.dot(p3[m], g_ref[0, m], preferred_element_type=F32)
            r = fold(r + jnp.dot(p3[m], e_ref[0, m], preferred_element_type=F32))
            for c in range(TILES):
                o_ref[m * TILES + c] = r[:, c * 128 : (c + 1) * 128]

    @pl.when(j >= STEPS)
    def _():
        o_ref[...] = jnp.zeros_like(o_ref)

    @pl.when(j == STEPS)
    def _():
        for m in range(MATS):
            p = psum_ref[m * 8 : (m + 1) * 8, :]
            gram = lax.dot_general(p, p, (((1,), (1,)), ((), ())), precision=lax.Precision.HIGHEST, preferred_element_type=F32)
            o_ref[m] = jnp.concatenate([gram, jnp.zeros((8, 120), F32)], axis=1)


def right(p_all, g, e):
    w_spec = pl.BlockSpec((1, MATS, ROWS, CHUNK), lambda j: (0, 0, 0, jnp.minimum(j, STEPS - 1)))
    return pl.pallas_call(
        right_kernel,
        grid=(N_DEV // (MATS * TILES),),
        in_specs=[pl.BlockSpec((N_DP, 16, ROWS), lambda j: (0, 0, 0)), w_spec, w_spec],
        out_specs=(pl.BlockSpec((MATS * TILES, 8, 128), lambda j: (j, 0, 0)), pl.BlockSpec((16, ROWS), lambda j: (0, 0))),
        out_shape=(jax.ShapeDtypeStruct((N_DEV, 8, 128), F32), jax.ShapeDtypeStruct((16, ROWS), F32)),
        scratch_shapes=[pltpu.VMEM((MATS, 24, ROWS), BF16)],
        compiler_params=pltpu.CompilerParams(vmem_limit_bytes=VMEM),
        name="right_factor",
    )(p_all, g, e)


def spread_kernel(t_ref, o_ref):
    total = jnp.sum(t_ref[...], axis=0, keepdims=True) * (1.0 / N_DP)
    o_ref[...] = jnp.broadcast_to(total, o_ref.shape)


def sum_everywhere(tiles):
    mine = lax.all_to_all(tiles, ALL, 0, 0)
    copies = pl.pallas_call(
        spread_kernel,
        out_shape=jax.ShapeDtypeStruct((N_DEV, 8, 128), F32),
        name="sum_tiles",
    )(mine)
    return lax.all_to_all(copies, ALL, 0, 0)


def final_kernel(g_ref, e_ref, z_ref, gram_ref, p_ref, a_ref, n_ref, q_ref, lower, p6):
    j = pl.program_id(0)

    @pl.when(j == 0)
    def _():
        for m in range(MATS):
            lower_inv = inverse_lower(gram_ref[m])
            lower[m] = jnp.concatenate([lower_inv, jnp.zeros((8, 120), F32)], axis=1)
            one, two, rest = split3(small_dot(lower_inv, p_ref[m * 8 : (m + 1) * 8, :]))
            pieces = jnp.concatenate([one, one, two, two, one, rest, jnp.zeros((80, ROWS), F32)], axis=0)
            pieces = jnp.concatenate([pieces, jnp.zeros((128, 64), F32)], axis=1)
            p6[m] = pieces.T.astype(BF16)

    for m in range(MATS):
        z = jnp.concatenate([z_ref[m * TILES + c] for c in range(TILES)], axis=1)
        q = small_dot(lower[m], z)
        q_ref[m] = q
        one, two, rest = split3(q)
        pieces = jnp.concatenate([one, two, one, two, rest, one], axis=0).astype(BF16)
        full = jnp.dot(p6[m, 0:ROWS, 0:48], pieces, preferred_element_type=F32)
        a_ref[m] = full.astype(BF16)
        n_ref[0, m] = (g_ref[0, m].astype(F32) + e_ref[0, m].astype(F32) - full).astype(BF16)


def final(g, e, z, p):
    w_spec = pl.BlockSpec((1, MATS, ROWS, CHUNK), lambda j: (0, 0, 0, j))
    return pl.pallas_call(
        final_kernel,
        grid=(STEPS,),
        in_specs=[w_spec, w_spec, pl.BlockSpec((MATS * TILES, 8, 128), lambda j: (j, 0, 0)),
                  pl.BlockSpec((MATS, 8, 128), lambda j: (GRAM // MATS, 0, 0)), pl.BlockSpec((16, ROWS), lambda j: (0, 0))],
        out_specs=(pl.BlockSpec((MATS, ROWS, CHUNK), lambda j: (0, 0, j)), w_spec,
                   pl.BlockSpec((MATS, RANK, CHUNK), lambda j: (0, 0, j))),
        out_shape=(jax.ShapeDtypeStruct((MATS, ROWS, COLS), BF16), jax.ShapeDtypeStruct((1, MATS, ROWS, COLS), BF16),
                   jax.ShapeDtypeStruct((MATS, RANK, COLS), F32)),
        scratch_shapes=[pltpu.VMEM((MATS, 8, 128), F32), pltpu.VMEM((MATS, 256, 128), BF16)],
        compiler_params=pltpu.CompilerParams(vmem_limit_bytes=VMEM),
        name="residual",
    )(g, e, z, z, p)


def everyones(p):
    return lax.all_to_all(jnp.broadcast_to(p[None], (N_DP,) + p.shape), "dp", 0, 0)


def per_device(grads, errors, q_init):
    p_own = left(grads, errors, jnp.swapaxes(q_init, 1, 2))
    tiles, _ = right(everyones(p_own), grads, errors)
    z = sum_everywhere(tiles)
    p_own = left(grads, errors, z, z)
    tiles, p = right(everyones(p_own), grads, errors)
    z = sum_everywhere(tiles)
    approx, errors_next, q_next = final(grads, errors, z, p)
    return approx, errors_next, jnp.swapaxes(q_next, 1, 2)


def solution(mesh):
    fine = Mesh(mesh.devices.reshape(4, 4, 4, 2), ALL)
    fsdp = ("x", "y", "core")
    in_specs = (P("dp", None, fsdp, None), P("dp", None, fsdp, None), P())
    out_specs = (P(None, fsdp, None), P("dp", None, fsdp, None), P())
    return jax.shard_map(per_device, mesh=fine, in_specs=in_specs, out_specs=out_specs, check_vma=False)
```

```python
import functools

import jax
import jax.numpy as jnp
from jax import lax
from jax.experimental import pallas as pl
from jax.experimental.pallas import tpu as pltpu
from jax.sharding import Mesh, PartitionSpec as P

F32, BF16 = jnp.float32, jnp.bfloat16
MATS, RANK, ROWS, COLS = 2, 8, 192, 6144
CHUNK = 1024
STEPS = COLS // CHUNK
TILES = CHUNK // 128
N_DP, PLANE = 4, 16
DEEP = COLS // 128 * RANK // PLANE
NT = (((1,), (1,)), ((), ()))
IN_VMEM = pl.BlockSpec(memory_space=pltpu.VMEM)
IN_SMEM = pl.BlockSpec(memory_space=pltpu.SMEM)
ANYWHERE = pl.BlockSpec(memory_space=pl.ANY)


def vmem(a):
    return pltpu.with_memory_space_constraint(a, pltpu.VMEM)


def hbm(a):
    return pltpu.with_memory_space_constraint(a, pltpu.HBM)


def kernel(body, out_shape, in_specs, name, scratch=(), limit=16, flops=10**7):
    many = isinstance(out_shape, tuple)
    out_specs = tuple(ANYWHERE if isinstance(s, jax.ShapeDtypeStruct) else IN_VMEM for s in (out_shape if many else (out_shape,)))
    return pl.pallas_call(
        body,
        in_specs=in_specs,
        out_specs=out_specs if many else out_specs[0],
        out_shape=out_shape,
        scratch_shapes=list(scratch),
        compiler_params=pltpu.CompilerParams(vmem_limit_bytes=limit * 1024 * 1024),
        cost_estimate=pl.CostEstimate(flops=flops, bytes_accessed=10**6, transcendentals=0),
        name=name,
    )


def split3(a):
    one = a.astype(BF16).astype(F32)
    rest = a - one
    two = rest.astype(BF16).astype(F32)
    return one, two, rest - two


def three(a):
    return jnp.concatenate(split3(a), axis=0).astype(BF16)


def fold(r):
    return r[0:8] + r[8:16] + r[16:24]


def small_dot(a, b):
    total = a[:, 0:1] * b[0:1, :]
    for k in range(1, RANK):
        total = total + a[:, k : k + 1] * b[k : k + 1, :]
    return total


def inverse_lower(gram):
    row = lax.broadcasted_iota(jnp.int32, (8, 128), 0)
    lane = lax.broadcasted_iota(jnp.int32, (8, 128), 1)
    a = jnp.where(lane < RANK, gram, jnp.where(lane == row + RANK, 1.0, 0.0).astype(F32))
    for k in range(RANK):
        pivot = a[k : k + 1, k : k + 1]
        inv = lax.rsqrt(pivot)
        inv = inv * (1.5 - 0.5 * pivot * inv * inv)
        top = a[k : k + 1, :] * inv
        below = a - (a[:, k : k + 1] * inv) * top
        a = jnp.where(row == k, top, jnp.where(row > k, below, a))
    return jnp.concatenate([a[:, RANK : 2 * RANK], jnp.zeros((8, 120), F32)], axis=1)


def chunk_of(q_ref, c):
    tiles = range(c * TILES, (c + 1) * TILES)
    return jnp.concatenate([q_ref[t // 3, t % 3 * 8 : t % 3 * 8 + 8, :] for t in tiles], axis=1)


def cols(c):
    return slice(c * CHUNK, (c + 1) * CHUNK)


def first_left_kernel(core_ref, g_hbm, e_hbm, q_ref, p_ref, g_ref, e_ref, g_sem, e_sem):
    core = core_ref[0]
    copies = []
    for c in range(STEPS):
        s = pl.ds(c * CHUNK, CHUNK)
        copies.append((
            pltpu.make_async_copy(g_hbm.at[0, :, :, s], g_ref.at[:, :, s], g_sem.at[c]),
            pltpu.make_async_copy(e_hbm.at[0, :, :, s], e_ref.at[:, :, s], e_sem.at[c]),
        ))
        copies[-1][0].start()
        copies[-1][1].start()
    acc = [jnp.zeros((24, ROWS), F32)] * MATS
    for c in range(STEPS):
        q = [three(q_ref[m, :, cols(c)]) for m in range(MATS)]
        copies[c][0].wait()
        copies[c][1].wait()
        for m in range(MATS):
            r = lax.dot_general(q[m], g_ref[m, :, cols(c)], NT, preferred_element_type=F32)
            r = r + lax.dot_general(q[m], e_ref[m, :, cols(c)], NT, preferred_element_type=F32)
            acc[m] = acc[m] + r
    for m in range(MATS):
        place = pl.multiple_of((m + core) % 2 * 8, 8)
        p_ref[pl.ds(place, 8), :] = fold(acc[m])


def first_left(core, grads, errors, q):
    wide = pltpu.VMEM((MATS, ROWS, COLS), BF16)
    return kernel(
        first_left_kernel, (pltpu.VMEM((16, ROWS), F32), wide, wide), [IN_SMEM, ANYWHERE, ANYWHERE, IN_VMEM], "first_left",
        [pltpu.SemaphoreType.DMA((STEPS,)), pltpu.SemaphoreType.DMA((STEPS,))],
    )(core, hbm(grads), hbm(errors), vmem(q))


def left_kernel(slot, core_ref, q_ref, g_ref, e_ref, *refs):
    p_ref = refs[-1]
    m = (core_ref[0] + slot) % 2
    acc = jnp.zeros((24, ROWS), F32)
    for c in range(STEPS):
        q = three(chunk_of(q_ref, c))
        acc = acc + lax.dot_general(q, g_ref[m, :, cols(c)], NT, preferred_element_type=F32)
        acc = acc + lax.dot_general(q, e_ref[m, :, cols(c)], NT, preferred_element_type=F32)
    if slot == 0:
        p_ref[...] = fold(acc)
    else:
        p_ref[0:8, :] = refs[0][...]
        p_ref[8:16, :] = fold(acc)


def left(core, q_own, q_other, g, e):
    own = kernel(functools.partial(left_kernel, 0), pltpu.VMEM((8, ROWS), F32), [IN_SMEM] + [IN_VMEM] * 3, "left_own", flops=10**9)(
        core, vmem(q_own), vmem(g), vmem(e))
    return kernel(functools.partial(left_kernel, 1), pltpu.VMEM((16, ROWS), F32), [IN_SMEM] + [IN_VMEM] * 4, "left_other")(
        core, vmem(q_other), vmem(g), vmem(e), vmem(own))


def right_kernel(slot, core_ref, p0, p1, p2, p3, g_ref, e_ref, o_ref, mean_ref):
    m = (core_ref[0] + slot) % 2
    mean_ref[...] = (p0[...] + p1[...] + p2[...] + p3[...]) * (1.0 / N_DP)
    p = mean_ref[slot * 8 : slot * 8 + 8, :]
    pieces = three(p)
    gram = lax.dot_general(p, p, NT, precision=lax.Precision.HIGHEST, preferred_element_type=F32)
    gram = jnp.concatenate([gram, jnp.zeros((8, 120), F32)], axis=1)
    for k in range(PLANE):
        o_ref[k, DEEP : DEEP + 8, :] = gram
    for c in range(STEPS):
        r = jnp.dot(pieces, g_ref[m, :, cols(c)], preferred_element_type=F32)
        r = fold(r + jnp.dot(pieces, e_ref[m, :, cols(c)], preferred_element_type=F32))
        for i in range(TILES):
            t = c * TILES + i
            o_ref[t // 3, t % 3 * 8 : t % 3 * 8 + 8, :] = r[:, i * 128 : (i + 1) * 128]


def right(slot, core, p_all, g, e):
    return kernel(
        functools.partial(right_kernel, slot), (pltpu.VMEM((PLANE, DEEP + 8, 128), F32), pltpu.VMEM((16, ROWS), F32)),
        [IN_SMEM] + [IN_VMEM] * 6, "right_own" if slot == 0 else "right_other", flops=10**9,
    )(core, *map(vmem, p_all), vmem(g), vmem(e))


def plane_sum_kernel(t_ref, z_ref, gram_ref):
    total = jnp.sum(t_ref[...], axis=0)
    z_ref[...] = total[0:DEEP]
    gram_ref[...] = total[DEEP : DEEP + 8]


def plane_sum(t):
    return kernel(plane_sum_kernel, (pltpu.VMEM((DEEP, 128), F32), pltpu.VMEM((8, 128), F32)), [IN_VMEM], "plane_sum")(vmem(t))


def lower_kernel(gram_ref, o_ref):
    o_ref[...] = inverse_lower(gram_ref[...])


def lower_inverse(gram):
    return kernel(lower_kernel, pltpu.VMEM((8, 128), F32), [IN_VMEM], "lower_inverse", flops=10**9)(vmem(gram))


def spread_kernel(z0, z1, z2, z3, lower_ref, o_ref):
    total = (z0[...] + z1[...] + z2[...] + z3[...]) * (1.0 / N_DP)
    lower = lower_ref[...]
    q = jnp.concatenate([small_dot(lower, total[i * 8 : i * 8 + 8]) for i in range(DEEP // 8)], axis=0)
    o_ref[...] = jnp.broadcast_to(q[None], o_ref.shape)


def spread(z_all, lower):
    return kernel(spread_kernel, pltpu.VMEM((PLANE, DEEP, 128), F32), [IN_VMEM] * 5, "spread")(*map(vmem, z_all), vmem(lower))


def final_kernel(core_ref, lower_own, lower_other, q_own, q_other, p_ref, g_ref, e_ref, a_hbm, n_hbm, q_hbm,
                 p6, a_buf, n_buf, q_buf, a_sem, n_sem, q_sem):
    copies = []
    for slot, (lower_ref, q_ref) in enumerate(((lower_own, q_own), (lower_other, q_other))):
        m = (core_ref[0] + slot) % 2
        one, two, rest = split3(small_dot(lower_ref[...], p_ref[slot * 8 : slot * 8 + 8, :]))
        pieces = jnp.concatenate([one, one, two, two, one, rest, jnp.zeros((80, ROWS), F32)], axis=0)
        pieces = jnp.concatenate([pieces, jnp.zeros((128, 64), F32)], axis=1)
        p6[slot] = pieces.T.astype(BF16)
        left_pieces = p6[slot, 0:ROWS, 0:48]
        for c in range(STEPS):
            q = chunk_of(q_ref, c)
            q_buf[slot, :, cols(c)] = q
            one, two, rest = split3(q)
            pieces = jnp.concatenate([one, two, one, two, rest, one], axis=0).astype(BF16)
            full = jnp.dot(left_pieces, pieces, preferred_element_type=F32)
            a_buf[slot, :, cols(c)] = full.astype(BF16)
            n_buf[slot, :, cols(c)] = (g_ref[m, :, cols(c)].astype(F32) + e_ref[m, :, cols(c)].astype(F32) - full).astype(BF16)
            s = pl.ds(c * CHUNK, CHUNK)
            i = slot * STEPS + c
            copies.append(pltpu.make_async_copy(a_buf.at[slot, :, s], a_hbm.at[m, :, s], a_sem.at[i]))
            copies.append(pltpu.make_async_copy(n_buf.at[slot, :, s], n_hbm.at[0, m, :, s], n_sem.at[i]))
            copies[-2].start()
            copies[-1].start()
        copies.append(pltpu.make_async_copy(q_buf.at[slot], q_hbm.at[m], q_sem.at[slot]))
        copies[-1].start()
    for copy in copies:
        copy.wait()


def final(core, lower_own, lower_other, q_own, q_other, p, g, e):
    n = MATS * STEPS
    return kernel(
        final_kernel,
        (jax.ShapeDtypeStruct((MATS, ROWS, COLS), BF16), jax.ShapeDtypeStruct((1, MATS, ROWS, COLS), BF16),
         jax.ShapeDtypeStruct((MATS, RANK, COLS), F32)),
        [IN_SMEM] + [IN_VMEM] * 7, "residual",
        [pltpu.VMEM((MATS, 256, 128), BF16), pltpu.VMEM((MATS, ROWS, COLS), BF16), pltpu.VMEM((MATS, ROWS, COLS), BF16),
         pltpu.VMEM((MATS, RANK, COLS), F32), pltpu.SemaphoreType.DMA((n,)), pltpu.SemaphoreType.DMA((n,)),
         pltpu.SemaphoreType.DMA((MATS,))],
        limit=24,
    )(core, *map(vmem, (lower_own, lower_other, q_own, q_other, p, g, e)))


def swap(a, axis, n, k):
    return lax.ppermute(a, axis, [(i, i ^ k) for i in range(n)])


def everyones(a):
    return (a,) + tuple(swap(a, "dp", N_DP, k) for k in (1, 2, 3))


def right_sum(core, p_own, g, e):
    p_all = everyones(p_own)
    theirs, _ = right(1, core, p_all, g, e)
    arrived = swap(theirs, "core", 2, 1)
    mine, p = right(0, core, p_all, g, e)
    z, gram = plane_sum(lax.all_to_all(mine + arrived, ("x", "y"), 0, 0))
    z_all = everyones(z)
    lower = lower_inverse(gram)
    return lax.all_to_all(spread(z_all, lower), ("x", "y"), 0, 0), lower, p


def per_device(grads, errors, q_init):
    core = lax.axis_index("core").astype(jnp.int32).reshape(1)
    p_own, g, e = first_left(core, grads, errors, jnp.swapaxes(q_init, 1, 2))
    q_own, _, _ = right_sum(core, p_own, g, e)
    p_own = left(core, q_own, swap(q_own, "core", 2, 1), g, e)
    q_own, lower, p = right_sum(core, p_own, g, e)
    lower_other = swap(lower, "core", 2, 1)
    approx, errors_next, q_next = final(core, lower, lower_other, q_own, swap(q_own, "core", 2, 1), p, g, e)
    return approx, errors_next, jnp.swapaxes(q_next, 1, 2)


def solution(mesh):
    fine = Mesh(mesh.devices.reshape(4, 4, 4, 2), ("dp", "x", "y", "core"))
    fsdp = ("x", "y", "core")
    in_specs = (P("dp", None, fsdp, None), P("dp", None, fsdp, None), P())
    out_specs = (P(None, fsdp, None), P("dp", None, fsdp, None), P())
    return jax.shard_map(per_device, mesh=fine, in_specs=in_specs, out_specs=out_specs, check_vma=False)
```

```python
import functools

import jax
import jax.numpy as jnp
from jax import lax
from jax.experimental import pallas as pl
from jax.experimental.pallas import tpu as pltpu
from jax.sharding import Mesh, PartitionSpec as P

F32, BF16 = jnp.float32, jnp.bfloat16
MATS, RANK, ROWS, COLS = 2, 8, 192, 6144
CHUNK = 1024
STEPS = COLS // CHUNK
SIDE = 4
QUARTER = COLS // SIDE
DEEP = QUARTER // 128 * RANK
NT = (((1,), (1,)), ((), ()))
IN_VMEM = pl.BlockSpec(memory_space=pltpu.VMEM)
IN_SMEM = pl.BlockSpec(memory_space=pltpu.SMEM)
ANYWHERE = pl.BlockSpec(memory_space=pl.ANY)


def vmem(a):
    return pltpu.with_memory_space_constraint(a, pltpu.VMEM)


def hbm(a):
    return pltpu.with_memory_space_constraint(a, pltpu.HBM)


def kernel(body, out_shape, in_specs, name, scratch=(), limit=16, flops=10**7):
    many = isinstance(out_shape, tuple)
    out_specs = tuple(ANYWHERE if isinstance(s, jax.ShapeDtypeStruct) else IN_VMEM for s in (out_shape if many else (out_shape,)))
    return pl.pallas_call(
        body,
        in_specs=in_specs,
        out_specs=out_specs if many else out_specs[0],
        out_shape=out_shape,
        scratch_shapes=list(scratch),
        compiler_params=pltpu.CompilerParams(vmem_limit_bytes=limit * 1024 * 1024),
        cost_estimate=pl.CostEstimate(flops=flops, bytes_accessed=10**6, transcendentals=0),
        name=name,
    )


def split3(a):
    one = a.astype(BF16).astype(F32)
    rest = a - one
    two = rest.astype(BF16).astype(F32)
    return one, two, rest - two


def three(a):
    return jnp.concatenate(split3(a), axis=0).astype(BF16)


def fold(r):
    return r[0:8] + r[8:16] + r[16:24]


def small_dot(a, b):
    total = a[:, 0:1] * b[0:1, :]
    for k in range(1, RANK):
        total = total + a[:, k : k + 1] * b[k : k + 1, :]
    return total


def inverse_lower(gram):
    row = lax.broadcasted_iota(jnp.int32, (8, 128), 0)
    lane = lax.broadcasted_iota(jnp.int32, (8, 128), 1)
    a = jnp.where(lane < RANK, gram, jnp.where(lane == row + RANK, 1.0, 0.0).astype(F32))
    for k in range(RANK):
        pivot = a[k : k + 1, k : k + 1]
        inv = lax.rsqrt(pivot)
        inv = inv * (1.5 - 0.5 * pivot * inv * inv)
        top = a[k : k + 1, :] * inv
        below = a - (a[:, k : k + 1] * inv) * top
        a = jnp.where(row == k, top, jnp.where(row > k, below, a))
    return jnp.concatenate([a[:, RANK : 2 * RANK], jnp.zeros((8, 120), F32)], axis=1)


def block_of(q_ref):
    return jnp.concatenate([q_ref[t * 8 : t * 8 + 8, :] for t in range(DEEP // 8)], axis=1)


def quarter(place_ref, k):
    return pl.ds(pl.multiple_of((place_ref[1] ^ k) * QUARTER, QUARTER), QUARTER)


def cols(c):
    return slice(c * CHUNK, (c + 1) * CHUNK)


def first_left_kernel(place_ref, g_hbm, e_hbm, q_ref, p_ref, g_ref, e_ref, g_sem, e_sem):
    core = place_ref[0]
    copies = []
    for c in range(STEPS):
        s = pl.ds(c * CHUNK, CHUNK)
        copies.append((
            pltpu.make_async_copy(g_hbm.at[0, :, :, s], g_ref.at[:, :, s], g_sem.at[c]),
            pltpu.make_async_copy(e_hbm.at[0, :, :, s], e_ref.at[:, :, s], e_sem.at[c]),
        ))
        copies[-1][0].start()
        copies[-1][1].start()
    acc = [jnp.zeros((24, ROWS), F32)] * MATS
    for c in range(STEPS):
        q = [three(q_ref[m, :, cols(c)]) for m in range(MATS)]
        copies[c][0].wait()
        copies[c][1].wait()
        for m in range(MATS):
            r = lax.dot_general(q[m], g_ref[m, :, cols(c)], NT, preferred_element_type=F32)
            r = r + lax.dot_general(q[m], e_ref[m, :, cols(c)], NT, preferred_element_type=F32)
            acc[m] = acc[m] + r
    for m in range(MATS):
        place = pl.multiple_of((m + core) % 2 * 8, 8)
        p_ref[pl.ds(place, 8), :] = fold(acc[m])


def first_left(place, grads, errors, q):
    wide = pltpu.VMEM((MATS, ROWS, COLS), BF16)
    return kernel(
        first_left_kernel, (pltpu.VMEM((16, ROWS), F32), wide, wide), [IN_SMEM, ANYWHERE, ANYWHERE, IN_VMEM], "first_left",
        [pltpu.SemaphoreType.DMA((STEPS,)), pltpu.SemaphoreType.DMA((STEPS,))],
    )(place, hbm(grads), hbm(errors), vmem(q))


def left_kernel(slot, place_ref, q0, q1, q2, q3, g_ref, e_ref, *refs):
    p_ref = refs[-1]
    m = (place_ref[0] + slot) % 2
    acc = jnp.zeros((24, ROWS), F32)
    for k, q_ref in enumerate((q0, q1, q2, q3)):
        q = three(block_of(q_ref))
        acc = acc + lax.dot_general(q, g_ref[m, :, quarter(place_ref, k)], NT, preferred_element_type=F32)
        acc = acc + lax.dot_general(q, e_ref[m, :, quarter(place_ref, k)], NT, preferred_element_type=F32)
    if slot == 0:
        p_ref[...] = fold(acc)
    else:
        p_ref[0:8, :] = refs[0][...]
        p_ref[8:16, :] = fold(acc)


def left(place, q_own, q_other, g, e):
    own = kernel(functools.partial(left_kernel, 0), pltpu.VMEM((8, ROWS), F32), [IN_SMEM] + [IN_VMEM] * 6, "left_own", flops=10**9)(
        place, *map(vmem, q_own), vmem(g), vmem(e))
    return kernel(functools.partial(left_kernel, 1), pltpu.VMEM((16, ROWS), F32), [IN_SMEM] + [IN_VMEM] * 7, "left_other")(
        place, *map(vmem, q_other), vmem(g), vmem(e), vmem(own))


def right_kernel(slot, place_ref, p0, p1, p2, p3, g_ref, e_ref, o_ref, *mean_ref):
    m = (place_ref[0] + slot) % 2
    p = ((p0[...] + p1[...]) + (p2[...] + p3[...])) * (1.0 / SIDE)
    if mean_ref:
        mean_ref[0][...] = p
    p = p[slot * 8 : slot * 8 + 8, :]
    pieces = three(p)
    gram = lax.dot_general(p, p, NT, precision=lax.Precision.HIGHEST, preferred_element_type=F32)
    gram = jnp.concatenate([gram, jnp.zeros((8, 120), F32)], axis=1)
    for k in range(SIDE):
        o_ref[k, DEEP : DEEP + 8, :] = gram
        s = slice(k * QUARTER, (k + 1) * QUARTER)
        r = jnp.dot(pieces, g_ref[m, :, s], preferred_element_type=F32)
        r = fold(r + jnp.dot(pieces, e_ref[m, :, s], preferred_element_type=F32))
        for t in range(DEEP // 8):
            o_ref[k, t * 8 : t * 8 + 8, :] = r[:, t * 128 : (t + 1) * 128]


def right(slot, place, p_all, g, e, keep=False):
    out = (pltpu.VMEM((SIDE, DEEP + 8, 128), F32),) + ((pltpu.VMEM((16, ROWS), F32),) if keep else ())
    return kernel(
        functools.partial(right_kernel, slot), out, [IN_SMEM] + [IN_VMEM] * 6, "right_own" if slot == 0 else "right_other", flops=10**9,
    )(place, *map(vmem, p_all), vmem(g), vmem(e))


def pick_kernel(place_ref, mine_ref, arrived_ref, *o_refs):
    for k, o_ref in enumerate(o_refs):
        o_ref[...] = mine_ref[place_ref[1] ^ k] + arrived_ref[place_ref[1] ^ k]


def pick(place, mine, arrived):
    return kernel(pick_kernel, (pltpu.VMEM((DEEP + 8, 128), F32),) * SIDE, [IN_SMEM] + [IN_VMEM] * 2, "pick")(
        place, vmem(mine), vmem(arrived))


def add_kernel(a, b, c, d, *o_refs):
    total = (a[...] + b[...]) + (c[...] + d[...])
    o_refs[0][...] = total[0 : o_refs[0].shape[0]]
    if len(o_refs) > 1:
        o_refs[1][...] = total[DEEP : DEEP + 8]


def add(parts, *rows):
    return kernel(add_kernel, tuple(pltpu.VMEM((r, 128), F32) for r in rows), [IN_VMEM] * SIDE, "add")(*map(vmem, parts))


def lower_kernel(gram_ref, o_ref):
    o_ref[...] = inverse_lower(gram_ref[...])


def lower_inverse(gram):
    return kernel(lower_kernel, pltpu.VMEM((8, 128), F32), [IN_VMEM], "lower_inverse", flops=10**9)(vmem(gram))


def normal_kernel(z0, z1, z2, z3, lower_ref, o_ref):
    total = ((z0[...] + z1[...]) + (z2[...] + z3[...])) * (1.0 / SIDE)
    lower = lower_ref[...]
    for t in range(DEEP // 8):
        o_ref[t * 8 : t * 8 + 8, :] = small_dot(lower, total[t * 8 : t * 8 + 8])


def normal(z_all, lower):
    return kernel(normal_kernel, pltpu.VMEM((DEEP, 128), F32), [IN_VMEM] * 5, "normal")(*map(vmem, z_all), vmem(lower))


def final_kernel(place_ref, lower_own, lower_other, *refs):
    q_refs, (p_ref, g_ref, e_ref, a_hbm, n_hbm, q_hbm, p6, a_buf, n_buf, q_buf, a_sem, n_sem, q_sem) = refs[:8], refs[8:]
    copies = []
    for slot, lower_ref in enumerate((lower_own, lower_other)):
        m = (place_ref[0] + slot) % 2
        one, two, rest = split3(small_dot(lower_ref[...], p_ref[slot * 8 : slot * 8 + 8, :]))
        pieces = jnp.concatenate([one, one, two, two, one, rest, jnp.zeros((80, ROWS), F32)], axis=0)
        pieces = jnp.concatenate([pieces, jnp.zeros((128, 64), F32)], axis=1)
        p6[slot] = pieces.T.astype(BF16)
        left_pieces = p6[slot, 0:ROWS, 0:48]
        for k in range(SIDE):
            i = slot * SIDE + k
            s = quarter(place_ref, k)
            q = block_of(q_refs[i])
            q_buf[i] = q
            one, two, rest = split3(q)
            pieces = jnp.concatenate([one, two, one, two, rest, one], axis=0).astype(BF16)
            full = jnp.dot(left_pieces, pieces, preferred_element_type=F32)
            a_buf[i] = full.astype(BF16)
            n_buf[i] = (g_ref[m, :, s].astype(F32) + e_ref[m, :, s].astype(F32) - full).astype(BF16)
            copies.append(pltpu.make_async_copy(a_buf.at[i], a_hbm.at[m, :, s], a_sem.at[i]))
            copies.append(pltpu.make_async_copy(n_buf.at[i], n_hbm.at[0, m, :, s], n_sem.at[i]))
            copies.append(pltpu.make_async_copy(q_buf.at[i], q_hbm.at[m, :, s], q_sem.at[i]))
            for copy in copies[-3:]:
                copy.start()
    for copy in copies:
        copy.wait()


def final(place, lower_own, lower_other, q_own, q_other, p, g, e):
    n = MATS * SIDE
    return kernel(
        final_kernel,
        (jax.ShapeDtypeStruct((MATS, ROWS, COLS), BF16), jax.ShapeDtypeStruct((1, MATS, ROWS, COLS), BF16),
         jax.ShapeDtypeStruct((MATS, RANK, COLS), F32)),
        [IN_SMEM] + [IN_VMEM] * 13, "residual",
        [pltpu.VMEM((MATS, 256, 128), BF16), pltpu.VMEM((n, ROWS, QUARTER), BF16), pltpu.VMEM((n, ROWS, QUARTER), BF16),
         pltpu.VMEM((n, RANK, QUARTER), F32)] + [pltpu.SemaphoreType.DMA((n,))] * 3,
        limit=24,
    )(place, *map(vmem, (lower_own, lower_other, *q_own, *q_other, p, g, e)))


def swap(a, axis, k):
    n = lax.axis_size(axis)
    return lax.ppermute(a, axis, [(i, i ^ k) for i in range(n)])


def everyones(a, axis):
    return (a,) + tuple(swap(a, axis, k) for k in (1, 2, 3))


def right_sum(place, p_own, g, e, keep):
    p_all = everyones(p_own, "dp")
    (theirs,) = right(1, place, p_all, g, e)
    arrived = swap(theirs, "core", 1)
    mine, *p = right(0, place, p_all, g, e, keep)
    parts = pick(place, mine, arrived)
    (z,) = add((parts[0],) + tuple(swap(parts[k], "x", k) for k in (1, 2, 3)), DEEP + 8)
    z, gram = add(everyones(z, "y"), DEEP, 8)
    z_all = everyones(z, "dp")
    lower = lower_inverse(gram)
    return everyones(normal(z_all, lower), "x"), lower, p


def per_device(grads, errors, q_init):
    place = jnp.stack([lax.axis_index("core"), lax.axis_index("x")]).astype(jnp.int32)
    p_own, g, e = first_left(place, grads, errors, jnp.swapaxes(q_init, 1, 2))
    q_own, _, _ = right_sum(place, p_own, g, e, False)
    p_own = left(place, q_own, [swap(q, "core", 1) for q in q_own], g, e)
    q_own, lower, (p,) = right_sum(place, p_own, g, e, True)
    q_other = [swap(q, "core", 1) for q in q_own]
    approx, errors_next, q_next = final(place, lower, swap(lower, "core", 1), q_own, q_other, p, g, e)
    return approx, errors_next, jnp.swapaxes(q_next, 1, 2)


def solution(mesh):
    fine = Mesh(mesh.devices.reshape(4, 4, 4, 2), ("dp", "x", "y", "core"))
    fsdp = ("x", "y", "core")
    in_specs = (P("dp", None, fsdp, None), P("dp", None, fsdp, None), P())
    out_specs = (P(None, fsdp, None), P("dp", None, fsdp, None), P())
    return jax.shard_map(per_device, mesh=fine, in_specs=in_specs, out_specs=out_specs, check_vma=False)
```

```python
import functools

import jax
import jax.numpy as jnp
from jax import lax
from jax.experimental import pallas as pl
from jax.experimental.pallas import tpu as pltpu
from jax.sharding import Mesh, PartitionSpec as P

F32, BF16 = jnp.float32, jnp.bfloat16
MATS, RANK, ROWS, COLS = 2, 8, 192, 6144
CHUNK = 1024
STEPS = COLS // CHUNK
SIDE = 4
QUARTER = COLS // SIDE
BLOCK = QUARTER // 2
DEEP = QUARTER // 128 * RANK
NT = (((1,), (1,)), ((), ()))
IN_VMEM = pl.BlockSpec(memory_space=pltpu.VMEM)
ANYWHERE = pl.BlockSpec(memory_space=pl.ANY)


def vmem(a):
    return pltpu.with_memory_space_constraint(a, pltpu.VMEM)


def hbm(a):
    return pltpu.with_memory_space_constraint(a, pltpu.HBM)


def kernel(body, out_shape, in_specs, name, scratch=(), limit=16, flops=10**7):
    many = isinstance(out_shape, tuple)
    out_specs = tuple(ANYWHERE if isinstance(s, jax.ShapeDtypeStruct) else IN_VMEM for s in (out_shape if many else (out_shape,)))
    return pl.pallas_call(
        body,
        in_specs=in_specs,
        out_specs=out_specs if many else out_specs[0],
        out_shape=out_shape,
        scratch_shapes=list(scratch),
        compiler_params=pltpu.CompilerParams(vmem_limit_bytes=limit * 1024 * 1024),
        cost_estimate=pl.CostEstimate(flops=flops, bytes_accessed=10**6, transcendentals=0),
        name=name,
    )


def split3(a):
    one = a.astype(BF16).astype(F32)
    rest = a - one
    two = rest.astype(BF16).astype(F32)
    return one, two, rest - two


def three(a):
    return jnp.concatenate(split3(a), axis=0).astype(BF16)


def fold(r):
    return r[0:8] + r[8:16] + r[16:24]


def small_dot(a, b):
    total = a[:, 0:1] * b[0:1, :]
    for k in range(1, RANK):
        total = total + a[:, k : k + 1] * b[k : k + 1, :]
    return total


def inverse_lower(gram):
    row = lax.broadcasted_iota(jnp.int32, (8, 128), 0)
    lane = lax.broadcasted_iota(jnp.int32, (8, 128), 1)
    a = jnp.where(lane < RANK, gram, jnp.where(lane == row + RANK, 1.0, 0.0).astype(F32))
    for k in range(RANK):
        pivot = a[k : k + 1, k : k + 1]
        inv = lax.rsqrt(pivot)
        inv = inv * (1.5 - 0.5 * pivot * inv * inv)
        top = a[k : k + 1, :] * inv
        below = a - (a[:, k : k + 1] * inv) * top
        a = jnp.where(row == k, top, jnp.where(row > k, below, a))
    return jnp.concatenate([a[:, RANK : 2 * RANK], jnp.zeros((8, 120), F32)], axis=1)


def block_of(q, h):
    tiles = range(h * (BLOCK // 128), (h + 1) * (BLOCK // 128))
    return jnp.concatenate([q[t * 8 : t * 8 + 8, :] for t in tiles], axis=1)


def half(k, h):
    return pl.ds(pl.multiple_of((lax.axis_index("x") ^ k) * QUARTER + h * BLOCK, BLOCK), BLOCK)


def cols(c):
    return slice(c * CHUNK, (c + 1) * CHUNK)


def first_left_kernel(g_hbm, e_hbm, q_hbm, p_ref, g_ref, e_ref, q_ref, g_sem, e_sem, q_sem):
    core = lax.axis_index("core")
    copies = []
    q_copy = pltpu.make_async_copy(q_hbm, q_ref, q_sem)
    q_copy.start()
    for c in range(STEPS):
        s = pl.ds(c * CHUNK, CHUNK)
        copies.append((
            pltpu.make_async_copy(g_hbm.at[0, :, :, s], g_ref.at[:, :, s], g_sem.at[c]),
            pltpu.make_async_copy(e_hbm.at[0, :, :, s], e_ref.at[:, :, s], e_sem.at[c]),
        ))
        copies[-1][0].start()
        copies[-1][1].start()
    acc = [jnp.zeros((24, ROWS), F32)] * MATS
    q_copy.wait()
    for c in range(STEPS):
        q = [three(q_ref[m, :, cols(c)]) for m in range(MATS)]
        copies[c][0].wait()
        copies[c][1].wait()
        for m in range(MATS):
            r = lax.dot_general(q[m], g_ref[m, :, cols(c)], NT, preferred_element_type=F32)
            r = r + lax.dot_general(q[m], e_ref[m, :, cols(c)], NT, preferred_element_type=F32)
            acc[m] = acc[m] + r
    for m in range(MATS):
        place = pl.multiple_of((core ^ m) * 8, 8)
        p_ref[pl.ds(place, 8), :] = fold(acc[m])


def first_left(grads, errors, q):
    wide = pltpu.VMEM((MATS, ROWS, COLS), BF16)
    return kernel(
        first_left_kernel, (pltpu.VMEM((16, ROWS), F32), wide, wide), [ANYWHERE] * 3, "first_left",
        [pltpu.VMEM((MATS, RANK, COLS), F32), pltpu.SemaphoreType.DMA((STEPS,)), pltpu.SemaphoreType.DMA((STEPS,)), pltpu.SemaphoreType.DMA],
    )(hbm(grads), hbm(errors), hbm(q))


def left_kernel(slot, q_ref, g_ref, e_ref, *refs):
    p_ref = refs[-1]
    m = lax.axis_index("core") ^ slot
    acc = jnp.zeros((24, ROWS), F32)
    for k in range(SIDE):
        for h in range(2):
            q = three(block_of(q_ref[k], h))
            acc = acc + lax.dot_general(q, g_ref[m, :, half(k, h)], NT, preferred_element_type=F32)
            acc = acc + lax.dot_general(q, e_ref[m, :, half(k, h)], NT, preferred_element_type=F32)
    if slot == 0:
        p_ref[...] = fold(acc)
    else:
        p_ref[0:8, :] = refs[0][...]
        p_ref[8:16, :] = fold(acc)


def left(q_own, q_other, g, e):
    own = kernel(functools.partial(left_kernel, 0), pltpu.VMEM((8, ROWS), F32), [IN_VMEM] * 3, "left_own", flops=10**9)(
        vmem(q_own), vmem(g), vmem(e))
    return kernel(functools.partial(left_kernel, 1), pltpu.VMEM((16, ROWS), F32), [IN_VMEM] * 4, "left_other")(
        vmem(q_other), vmem(g), vmem(e), vmem(own))


def right_kernel(slot, p0, p1, p2, p3, g_ref, e_ref, o_ref, *mean_ref):
    m = lax.axis_index("core") ^ slot
    p = ((p0[...] + p1[...]) + (p2[...] + p3[...])) * (1.0 / SIDE)
    if mean_ref:
        mean_ref[0][...] = p
    p = p[slot * 8 : slot * 8 + 8, :]
    pieces = three(p)
    gram = lax.dot_general(p, p, NT, precision=lax.Precision.HIGHEST, preferred_element_type=F32)
    gram = jnp.concatenate([gram, jnp.zeros((8, 120), F32)], axis=1)
    for k in range(SIDE):
        o_ref[k, DEEP : DEEP + 8, :] = gram
        for h in range(2):
            s = slice(k * QUARTER + h * BLOCK, k * QUARTER + (h + 1) * BLOCK)
            r = jnp.dot(pieces, g_ref[m, :, s], preferred_element_type=F32)
            r = fold(r + jnp.dot(pieces, e_ref[m, :, s], preferred_element_type=F32))
            for i in range(BLOCK // 128):
                t = h * (BLOCK // 128) + i
                o_ref[k, t * 8 : t * 8 + 8, :] = r[:, i * 128 : (i + 1) * 128]


def right(slot, p_all, g, e, keep=False):
    out = (pltpu.VMEM((SIDE, DEEP + 8, 128), F32),) + ((pltpu.VMEM((16, ROWS), F32),) if keep else ())
    return kernel(
        functools.partial(right_kernel, slot), out, [IN_VMEM] * 6, "right_own" if slot == 0 else "right_other", flops=10**9,
    )(*map(vmem, p_all), vmem(g), vmem(e))


def pick_kernel(mine_ref, arrived_ref, *o_refs):
    for k, o_ref in enumerate(o_refs):
        o_ref[...] = mine_ref[lax.axis_index("x") ^ k] + arrived_ref[lax.axis_index("x") ^ k]


def pick(mine, arrived):
    return kernel(pick_kernel, (pltpu.VMEM((DEEP + 8, 128), F32),) * SIDE, [IN_VMEM] * 2, "pick")(
        vmem(mine), vmem(arrived))


def add_kernel(a, b, c, d, *o_refs):
    total = (a[...] + b[...]) + (c[...] + d[...])
    o_refs[0][...] = total[0 : o_refs[0].shape[0]]
    if len(o_refs) > 1:
        o_refs[1][...] = total[DEEP : DEEP + 8]


def add(parts, *rows):
    return kernel(add_kernel, tuple(pltpu.VMEM((r, 128), F32) for r in rows), [IN_VMEM] * SIDE, "add")(*map(vmem, parts))


def lower_kernel(gram_ref, o_ref):
    o_ref[...] = inverse_lower(gram_ref[...])


def lower_inverse(gram):
    return kernel(lower_kernel, pltpu.VMEM((8, 128), F32), [IN_VMEM], "lower_inverse", flops=10**9)(vmem(gram))


def normal_kernel(z0, z1, z2, z3, lower_ref, o_ref):
    total = ((z0[...] + z1[...]) + (z2[...] + z3[...])) * (1.0 / SIDE)
    lower = lower_ref[...]
    for t in range(DEEP // 8):
        o_ref[t * 8 : t * 8 + 8, :] = small_dot(lower, total[t * 8 : t * 8 + 8])


def normal(z_all, lower):
    return kernel(normal_kernel, pltpu.VMEM((DEEP, 128), F32), [IN_VMEM] * 5, "normal")(*map(vmem, z_all), vmem(lower))


def join_kernel(q0, q1, q2, q3, o_ref):
    for k, q_ref in enumerate((q0, q1, q2, q3)):
        o_ref[k] = q_ref[...]


def join(parts):
    return kernel(join_kernel, pltpu.VMEM((SIDE, DEEP, 128), F32), [IN_VMEM] * SIDE, "join")(*map(vmem, parts))


def final_kernel(lower_own, lower_other, q_own, q_other, p_ref, g_ref, e_ref, a_hbm, n_hbm, q_hbm,
                 p6, a_buf, n_buf, q_buf, a_sem, n_sem, q_sem):
    copies = []
    for slot, (lower_ref, q_ref) in enumerate(((lower_own, q_own), (lower_other, q_other))):
        m = lax.axis_index("core") ^ slot
        one, two, rest = split3(small_dot(lower_ref[...], p_ref[slot * 8 : slot * 8 + 8, :]))
        pieces = jnp.concatenate([one, one, two, two, one, rest, jnp.zeros((80, ROWS), F32)], axis=0)
        pieces = jnp.concatenate([pieces, jnp.zeros((128, 64), F32)], axis=1)
        p6[slot] = pieces.T.astype(BF16)
        left_pieces = p6[slot, 0:ROWS, 0:48]
        for k in range(SIDE):
            for h in range(2):
                i = (slot * SIDE + k) * 2 + h
                s = half(k, h)
                q = block_of(q_ref[k], h)
                q_buf[i] = q
                one, two, rest = split3(q)
                pieces = jnp.concatenate([one, two, one, two, rest, one], axis=0).astype(BF16)
                full = jnp.dot(left_pieces, pieces, preferred_element_type=F32)
                a_buf[i] = full.astype(BF16)
                n_buf[i] = (g_ref[m, :, s].astype(F32) + e_ref[m, :, s].astype(F32) - full).astype(BF16)
                copies.append(pltpu.make_async_copy(a_buf.at[i], a_hbm.at[m, :, s], a_sem.at[i]))
                copies.append(pltpu.make_async_copy(n_buf.at[i], n_hbm.at[0, m, :, s], n_sem.at[i]))
                copies.append(pltpu.make_async_copy(q_buf.at[i], q_hbm.at[m, :, s], q_sem.at[i]))
                for copy in copies[-3:]:
                    copy.start()
    for copy in copies:
        copy.wait()


def final(lower_own, lower_other, q_own, q_other, p, g, e):
    n = MATS * SIDE * 2
    return kernel(
        final_kernel,
        (jax.ShapeDtypeStruct((MATS, ROWS, COLS), BF16), jax.ShapeDtypeStruct((1, MATS, ROWS, COLS), BF16),
         jax.ShapeDtypeStruct((MATS, RANK, COLS), F32)),
        [IN_VMEM] * 7, "residual",
        [pltpu.VMEM((MATS, 256, 128), BF16), pltpu.VMEM((n, ROWS, BLOCK), BF16), pltpu.VMEM((n, ROWS, BLOCK), BF16),
         pltpu.VMEM((n, RANK, BLOCK), F32)] + [pltpu.SemaphoreType.DMA((n,))] * 3,
        limit=24,
    )(*map(vmem, (lower_own, lower_other, q_own, q_other, p, g, e)))


def swap(a, axis, k):
    n = lax.axis_size(axis)
    return lax.ppermute(a, axis, [(i, i ^ k) for i in range(n)])


def everyones(a, axis):
    return (a,) + tuple(swap(a, axis, k) for k in (1, 2, 3))


def right_sum(p_own, g, e, keep):
    p_all = everyones(p_own, "dp")
    (theirs,) = right(1, p_all, g, e)
    arrived = swap(theirs, "core", 1)
    mine, *p = right(0, p_all, g, e, keep)
    parts = pick(mine, arrived)
    (z,) = add((parts[0],) + tuple(swap(parts[k], "x", k) for k in (1, 2, 3)), DEEP + 8)
    z, gram = add(everyones(z, "y"), DEEP, 8)
    z_all = everyones(z, "dp")
    lower = lower_inverse(gram)
    return join(everyones(normal(z_all, lower), "x")), lower, p


def per_device(grads, errors, q_init):
    p_own, g, e = first_left(grads, errors, jnp.swapaxes(q_init, 1, 2))
    q_own, _, _ = right_sum(p_own, g, e, False)
    p_own = left(q_own, swap(q_own, "core", 1), g, e)
    q_own, lower, (p,) = right_sum(p_own, g, e, True)
    approx, errors_next, q_next = final(lower, swap(lower, "core", 1), q_own, swap(q_own, "core", 1), p, g, e)
    return approx, errors_next, jnp.swapaxes(q_next, 1, 2)


def solution(mesh):
    fine = Mesh(mesh.devices.reshape(4, 4, 4, 2), ("dp", "x", "y", "core"))
    fsdp = ("x", "y", "core")
    in_specs = (P("dp", None, fsdp, None), P("dp", None, fsdp, None), P())
    out_specs = (P(None, fsdp, None), P("dp", None, fsdp, None), P())
    return jax.shard_map(per_device, mesh=fine, in_specs=in_specs, out_specs=out_specs, check_vma=False)
```

```python
import functools

import jax
import jax.numpy as jnp
from jax import lax
from jax.experimental import pallas as pl
from jax.experimental.pallas import tpu as pltpu
from jax.sharding import Mesh, PartitionSpec as P

F32, BF16 = jnp.float32, jnp.bfloat16
MATS, RANK, ROWS, COLS = 2, 8, 192, 6144
CHUNK = 1024
STEPS = COLS // CHUNK
SIDE = 4
QUARTER = COLS // SIDE
BLOCK = QUARTER // 2
DEEP = QUARTER // 128 * RANK
NT = (((1,), (1,)), ((), ()))
IN_VMEM = pl.BlockSpec(memory_space=pltpu.VMEM)
ANYWHERE = pl.BlockSpec(memory_space=pl.ANY)


def vmem(a):
    return pltpu.with_memory_space_constraint(a, pltpu.VMEM)


def hbm(a):
    return pltpu.with_memory_space_constraint(a, pltpu.HBM)


def kernel(body, out_shape, in_specs, name, scratch=(), limit=16, flops=10**7):
    many = isinstance(out_shape, tuple)
    out_specs = tuple(ANYWHERE if isinstance(s, jax.ShapeDtypeStruct) else IN_VMEM for s in (out_shape if many else (out_shape,)))
    return pl.pallas_call(
        body,
        in_specs=in_specs,
        out_specs=out_specs if many else out_specs[0],
        out_shape=out_shape,
        scratch_shapes=list(scratch),
        compiler_params=pltpu.CompilerParams(vmem_limit_bytes=limit * 1024 * 1024),
        cost_estimate=pl.CostEstimate(flops=flops, bytes_accessed=10**6, transcendentals=0),
        name=name,
    )


def split3(a):
    one = a.astype(BF16).astype(F32)
    rest = a - one
    two = rest.astype(BF16).astype(F32)
    return one, two, rest - two


def three(a):
    return jnp.concatenate(split3(a), axis=0).astype(BF16)


def fold(r):
    return r[0:8] + r[8:16] + r[16:24]


def small_dot(a, b):
    total = a[:, 0:1] * b[0:1, :]
    for k in range(1, RANK):
        total = total + a[:, k : k + 1] * b[k : k + 1, :]
    return total


def inverse_lower(gram):
    row = lax.broadcasted_iota(jnp.int32, (8, 128), 0)
    lane = lax.broadcasted_iota(jnp.int32, (8, 128), 1)
    a = jnp.where(lane < RANK, gram, jnp.where(lane == row + RANK, 1.0, 0.0).astype(F32))
    for k in range(RANK):
        pivot = a[k : k + 1, k : k + 1]
        inv = lax.rsqrt(pivot)
        inv = inv * (1.5 - 0.5 * pivot * inv * inv)
        top = a[k : k + 1, :] * inv
        below = a - (a[:, k : k + 1] * inv) * top
        a = jnp.where(row == k, top, jnp.where(row > k, below, a))
    return jnp.concatenate([a[:, RANK : 2 * RANK], jnp.zeros((8, 120), F32)], axis=1)


def block_of(q_ref, k, h):
    first = k * DEEP + h * (BLOCK // 128) * 8
    return jnp.concatenate([q_ref[first + i * 8 : first + i * 8 + 8, :] for i in range(BLOCK // 128)], axis=1)


def half(k, h):
    return pl.ds(pl.multiple_of((lax.axis_index("x") ^ k) * QUARTER + h * BLOCK, BLOCK), BLOCK)


def matrix(slot):
    parity = lax.axis_index("x") ^ lax.axis_index("y") ^ lax.axis_index("dp")
    return lax.axis_index("core") ^ (parity & 1) ^ slot


def rows(m):
    return pl.ds(pl.multiple_of(m * 8, 8), 8)


def cols(c):
    return slice(c * CHUNK, (c + 1) * CHUNK)


def first_left_kernel(g_hbm, e_hbm, q_hbm, p_ref, g_ref, e_ref, q_ref, g_sem, e_sem, q_sem):
    copies = []
    for c in range(STEPS):
        s = pl.ds(c * CHUNK, CHUNK)
        copies.append((
            pltpu.make_async_copy(q_hbm.at[:, :, s], q_ref.at[:, :, s], q_sem.at[c]),
            pltpu.make_async_copy(g_hbm.at[0, :, :, s], g_ref.at[:, :, s], g_sem.at[c]),
            pltpu.make_async_copy(e_hbm.at[0, :, :, s], e_ref.at[:, :, s], e_sem.at[c]),
        ))
        for copy in copies[c]:
            copy.start()
    acc = [jnp.zeros((24, ROWS), F32)] * MATS
    for c in range(STEPS):
        copies[c][0].wait()
        q = [three(q_ref[m, :, cols(c)]) for m in range(MATS)]
        copies[c][1].wait()
        copies[c][2].wait()
        for m in range(MATS):
            r = lax.dot_general(q[m], g_ref[m, :, cols(c)], NT, preferred_element_type=F32)
            r = r + lax.dot_general(q[m], e_ref[m, :, cols(c)], NT, preferred_element_type=F32)
            acc[m] = acc[m] + r
    for m in range(MATS):
        p_ref[m * 8 : m * 8 + 8, :] = fold(acc[m])


def first_left(grads, errors, q):
    wide = pltpu.VMEM((MATS, ROWS, COLS), BF16)
    return kernel(
        first_left_kernel, (pltpu.VMEM((16, ROWS), F32), wide, wide), [ANYWHERE] * 3, "first_left",
        [pltpu.VMEM((MATS, RANK, COLS), F32)] + [pltpu.SemaphoreType.DMA((STEPS,))] * 3,
    )(hbm(grads), hbm(errors), hbm(q))


def left_kernel(slot, q_ref, g_ref, e_ref, *refs):
    p_ref = refs[-1]
    m = matrix(slot)
    acc = jnp.zeros((24, ROWS), F32)
    for k in range(SIDE):
        for h in range(2):
            q = three(block_of(q_ref, k, h))
            acc = acc + lax.dot_general(q, g_ref[m, :, half(k, h)], NT, preferred_element_type=F32)
            acc = acc + lax.dot_general(q, e_ref[m, :, half(k, h)], NT, preferred_element_type=F32)
    if slot == 0:
        p_ref[...] = fold(acc)
    else:
        p_ref[rows(matrix(0)), :] = refs[0][...]
        p_ref[rows(m), :] = fold(acc)


def left(q_own, q_other, g, e):
    own = kernel(functools.partial(left_kernel, 0), pltpu.VMEM((8, ROWS), F32), [IN_VMEM] * 3, "left_own", flops=10**9)(
        vmem(q_own), vmem(g), vmem(e))
    return kernel(functools.partial(left_kernel, 1), pltpu.VMEM((16, ROWS), F32), [IN_VMEM] * 4, "left_other")(
        vmem(q_other), vmem(g), vmem(e), vmem(own))


def right_kernel(slot, p0, p1, p2, p3, g_ref, e_ref, o_ref, *mean_ref):
    m = matrix(slot)
    p = ((p0[...] + p1[...]) + (p2[...] + p3[...])) * (1.0 / SIDE)
    if mean_ref:
        mean_ref[0][...] = p
    p = jnp.where(m == 0, p[0:8], p[8:16])
    pieces = three(p)
    gram = lax.dot_general(p, p, NT, precision=lax.Precision.HIGHEST, preferred_element_type=F32)
    gram = jnp.concatenate([gram, jnp.zeros((8, 120), F32)], axis=1)
    for k in range(SIDE):
        o_ref[k, DEEP : DEEP + 8, :] = gram
        for h in range(2):
            s = slice(k * QUARTER + h * BLOCK, k * QUARTER + (h + 1) * BLOCK)
            r = jnp.dot(pieces, g_ref[m, :, s], preferred_element_type=F32)
            r = fold(r + jnp.dot(pieces, e_ref[m, :, s], preferred_element_type=F32))
            for i in range(BLOCK // 128):
                t = h * (BLOCK // 128) + i
                o_ref[k, t * 8 : t * 8 + 8, :] = r[:, i * 128 : (i + 1) * 128]


def right(slot, p_all, g, e, keep=False):
    out = (pltpu.VMEM((SIDE, DEEP + 8, 128), F32),) + ((pltpu.VMEM((16, ROWS), F32),) if keep else ())
    return kernel(
        functools.partial(right_kernel, slot), out, [IN_VMEM] * 6, "right_own" if slot == 0 else "right_other", flops=10**9,
    )(*map(vmem, p_all), vmem(g), vmem(e))


def pick_kernel(mine_ref, arrived_ref, *o_refs):
    for k, o_ref in enumerate(o_refs):
        o_ref[...] = mine_ref[lax.axis_index("x") ^ k] + arrived_ref[lax.axis_index("x") ^ k]


def pick(mine, arrived):
    return kernel(pick_kernel, (pltpu.VMEM((DEEP + 8, 128), F32),) * SIDE, [IN_VMEM] * 2, "pick")(
        vmem(mine), vmem(arrived))


def add_kernel(a, b, c, d, *o_refs):
    total = (a[...] + b[...]) + (c[...] + d[...])
    o_refs[0][...] = total[0 : o_refs[0].shape[0]]
    if len(o_refs) > 1:
        o_refs[1][...] = total[DEEP : DEEP + 8]


def add(parts, *rows):
    return kernel(add_kernel, tuple(pltpu.VMEM((r, 128), F32) for r in rows), [IN_VMEM] * SIDE, "add")(*map(vmem, parts))


def lower_kernel(gram_ref, o_ref):
    o_ref[...] = inverse_lower(gram_ref[...])


def lower_inverse(gram):
    return kernel(lower_kernel, pltpu.VMEM((8, 128), F32), [IN_VMEM], "lower_inverse", flops=10**9)(vmem(gram))


def normal_kernel(z0, z1, z2, z3, lower_ref, o_ref):
    total = ((z0[...] + z1[...]) + (z2[...] + z3[...])) * (1.0 / SIDE)
    lower = lower_ref[...]
    for t in range(DEEP // 8):
        o_ref[t * 8 : t * 8 + 8, :] = small_dot(lower, total[t * 8 : t * 8 + 8])


def normal(z_all, lower):
    return kernel(normal_kernel, pltpu.VMEM((DEEP, 128), F32), [IN_VMEM] * 5, "normal")(*map(vmem, z_all), vmem(lower))


def join_kernel(q0, q1, q2, q3, lower_ref, o_ref):
    for k, q_ref in enumerate((q0, q1, q2, q3)):
        o_ref[k * DEEP : (k + 1) * DEEP, :] = q_ref[...]
    o_ref[SIDE * DEEP :, :] = lower_ref[...]


def join(parts, lower):
    return kernel(join_kernel, pltpu.VMEM((SIDE * DEEP + 8, 128), F32), [IN_VMEM] * 5, "join")(*map(vmem, parts), vmem(lower))


def final_kernel(slot, q_ref, p_ref, g_ref, e_ref, *refs):
    a_hbm, n_hbm, q_hbm, p6, a_buf, n_buf, q_buf, a_sem, n_sem, q_sem = refs[-10:]
    m = matrix(slot)
    copies = []
    one, two, rest = split3(small_dot(q_ref[SIDE * DEEP :, :], p_ref[rows(m), :]))
    pieces = jnp.concatenate([one, one, two, two, one, rest, jnp.zeros((80, ROWS), F32)], axis=0)
    pieces = jnp.concatenate([pieces, jnp.zeros((128, 64), F32)], axis=1)
    p6[...] = pieces.T.astype(BF16)
    left_pieces = p6[0:ROWS, 0:48]
    for k in range(SIDE):
        for h in range(2):
            i = k * 2 + h
            s = half(k, h)
            q = block_of(q_ref, k, h)
            q_buf[i] = q
            one, two, rest = split3(q)
            pieces = jnp.concatenate([one, two, one, two, rest, one], axis=0).astype(BF16)
            full = jnp.dot(left_pieces, pieces, preferred_element_type=F32)
            a_buf[i] = full.astype(BF16)
            n_buf[i] = (g_ref[m, :, s].astype(F32) + e_ref[m, :, s].astype(F32) - full).astype(BF16)
            copies.append(pltpu.make_async_copy(a_buf.at[i], a_hbm.at[m, :, s], a_sem.at[i]))
            copies.append(pltpu.make_async_copy(n_buf.at[i], n_hbm.at[0, m, :, s], n_sem.at[i]))
            copies.append(pltpu.make_async_copy(q_buf.at[i], q_hbm.at[m, :, s], q_sem.at[i]))
            for copy in copies[-3:]:
                copy.start()
    for copy in copies:
        copy.wait()


def final(slot, q, p, g, e, before=()):
    n = SIDE * 2
    return pl.pallas_call(
        functools.partial(final_kernel, slot),
        in_specs=[IN_VMEM] * 4 + [ANYWHERE] * len(before),
        out_specs=(ANYWHERE,) * 3,
        out_shape=(jax.ShapeDtypeStruct((MATS, ROWS, COLS), BF16), jax.ShapeDtypeStruct((1, MATS, ROWS, COLS), BF16),
                   jax.ShapeDtypeStruct((MATS, RANK, COLS), F32)),
        scratch_shapes=[pltpu.VMEM((256, 128), BF16), pltpu.VMEM((n, ROWS, BLOCK), BF16), pltpu.VMEM((n, ROWS, BLOCK), BF16),
                        pltpu.VMEM((n, RANK, BLOCK), F32)] + [pltpu.SemaphoreType.DMA((n,))] * 3,
        input_output_aliases={4 + i: i for i in range(len(before))},
        compiler_params=pltpu.CompilerParams(vmem_limit_bytes=16 * 1024 * 1024),
        cost_estimate=pl.CostEstimate(flops=10**9, bytes_accessed=10**7, transcendentals=0),
        name="residual_own" if slot == 0 else "residual_other",
    )(*map(vmem, (q, p, g, e)), *before)


def swap(a, axis, k):
    return lax.ppermute(a, axis, [(i, i ^ k) for i in range(lax.axis_size(axis))])


def cross(a, axis, k):
    return lax.ppermute(a, (axis, "core"), [(i * 2 + c, (i ^ k) * 2 + (c ^ (k & 1))) for i in range(SIDE) for c in range(2)])


def everyones(a, axis, move):
    return (a,) + tuple(move(a, axis, k) for k in (1, 2, 3))


def right_sum(p_own, g, e, keep):
    p_all = everyones(p_own, "dp", swap)
    (theirs,) = right(1, p_all, g, e)
    arrived = swap(theirs, "core", 1)
    mine, *p = right(0, p_all, g, e, keep)
    parts = pick(mine, arrived)
    (z,) = add((parts[0],) + tuple(cross(parts[k], "x", k) for k in (1, 2, 3)), DEEP + 8)
    z, gram = add(everyones(z, "y", cross), DEEP, 8)
    z_all = everyones(z, "dp", cross)
    lower = lower_inverse(gram)
    return join(everyones(normal(z_all, lower), "x", cross), lower), p


def per_device(grads, errors, q_init):
    p_own, g, e = first_left(grads, errors, jnp.swapaxes(q_init, 1, 2))
    q_own, _ = right_sum(p_own, g, e, False)
    p_own = left(q_own, swap(q_own, "core", 1), g, e)
    q_own, (p,) = right_sum(p_own, g, e, True)
    q_other = swap(q_own, "core", 1)
    approx, errors_next, q_next = final(1, q_other, p, g, e, final(0, q_own, p, g, e))
    return approx, errors_next, jnp.swapaxes(q_next, 1, 2)


def solution(mesh):
    fine = Mesh(mesh.devices.reshape(4, 4, 4, 2), ("dp", "x", "y", "core"))
    fsdp = ("x", "y", "core")
    in_specs = (P("dp", None, fsdp, None), P("dp", None, fsdp, None), P())
    out_specs = (P(None, fsdp, None), P("dp", None, fsdp, None), P())
    return jax.shard_map(per_device, mesh=fine, in_specs=in_specs, out_specs=out_specs, check_vma=False)
```

```python
import functools

import jax
import jax.numpy as jnp
from jax import lax
from jax.experimental import pallas as pl
from jax.experimental.pallas import tpu as pltpu
from jax.sharding import Mesh, PartitionSpec as P

F32, BF16 = jnp.float32, jnp.bfloat16
MATS, RANK, ROWS, COLS = 2, 8, 192, 6144
CHUNK = 1024
STEPS = COLS // CHUNK
SIDE = 4
QUARTER = COLS // SIDE
BLOCK = QUARTER // 2
DEEP = QUARTER // 128 * RANK
NT = (((1,), (1,)), ((), ()))
IN_VMEM = pl.BlockSpec(memory_space=pltpu.VMEM)
ANYWHERE = pl.BlockSpec(memory_space=pl.ANY)


def vmem(a):
    return pltpu.with_memory_space_constraint(a, pltpu.VMEM)


def hbm(a):
    return pltpu.with_memory_space_constraint(a, pltpu.HBM)


def kernel(body, out_shape, in_specs, name, scratch=(), limit=16, flops=10**7):
    many = isinstance(out_shape, tuple)
    out_specs = tuple(ANYWHERE if isinstance(s, jax.ShapeDtypeStruct) else IN_VMEM for s in (out_shape if many else (out_shape,)))
    return pl.pallas_call(
        body,
        in_specs=in_specs,
        out_specs=out_specs if many else out_specs[0],
        out_shape=out_shape,
        scratch_shapes=list(scratch),
        compiler_params=pltpu.CompilerParams(vmem_limit_bytes=limit * 1024 * 1024),
        cost_estimate=pl.CostEstimate(flops=flops, bytes_accessed=10**6, transcendentals=0),
        name=name,
    )


def split3(a):
    one = a.astype(BF16).astype(F32)
    rest = a - one
    two = rest.astype(BF16).astype(F32)
    return one, two, rest - two


def three(a):
    return jnp.concatenate(split3(a), axis=0).astype(BF16)


def fold(r):
    return r[0:8] + r[8:16] + r[16:24]


def small_dot(a, b):
    total = a[:, 0:1] * b[0:1, :]
    for k in range(1, RANK):
        total = total + a[:, k : k + 1] * b[k : k + 1, :]
    return total


def inverse_lower(gram):
    row = lax.broadcasted_iota(jnp.int32, (8, 128), 0)
    lane = lax.broadcasted_iota(jnp.int32, (8, 128), 1)
    a = jnp.where(lane < RANK, gram, jnp.where(lane == row + RANK, 1.0, 0.0).astype(F32))
    for k in range(RANK):
        pivot = a[k : k + 1, k : k + 1]
        inv = lax.rsqrt(pivot)
        inv = inv * (1.5 - 0.5 * pivot * inv * inv)
        top = a[k : k + 1, :] * inv
        below = a - (a[:, k : k + 1] * inv) * top
        a = jnp.where(row == k, top, jnp.where(row > k, below, a))
    return jnp.concatenate([a[:, RANK : 2 * RANK], jnp.zeros((8, 120), F32)], axis=1)


def block_of(q_ref, k, h):
    first = k * DEEP + h * (BLOCK // 128) * 8
    return jnp.concatenate([q_ref[first + i * 8 : first + i * 8 + 8, :] for i in range(BLOCK // 128)], axis=1)


def half(k, h):
    return pl.ds(pl.multiple_of((lax.axis_index("x") ^ k) * QUARTER + h * BLOCK, BLOCK), BLOCK)


def matrix(slot):
    parity = lax.axis_index("x") ^ lax.axis_index("y") ^ lax.axis_index("dp")
    return lax.axis_index("core") ^ (parity & 1) ^ slot


def rows(m):
    return pl.ds(pl.multiple_of(m * 8, 8), 8)


def cols(c):
    return slice(c * CHUNK, (c + 1) * CHUNK)


def first_left_kernel(g_hbm, e_hbm, q_hbm, p_ref, g_ref, e_ref, q_ref, g_sem, e_sem, q_sem):
    copies = []
    for c in range(STEPS):
        s = pl.ds(c * CHUNK, CHUNK)
        copies.append((
            pltpu.make_async_copy(q_hbm.at[:, :, s], q_ref.at[:, :, s], q_sem.at[c]),
            pltpu.make_async_copy(g_hbm.at[0, :, :, s], g_ref.at[:, :, s], g_sem.at[c]),
            pltpu.make_async_copy(e_hbm.at[0, :, :, s], e_ref.at[:, :, s], e_sem.at[c]),
        ))
        for copy in copies[c]:
            copy.start()
    acc = [jnp.zeros((24, ROWS), F32)] * MATS
    for c in range(STEPS):
        copies[c][0].wait()
        q = [three(q_ref[m, :, cols(c)]) for m in range(MATS)]
        copies[c][1].wait()
        copies[c][2].wait()
        for m in range(MATS):
            r = lax.dot_general(q[m], g_ref[m, :, cols(c)], NT, preferred_element_type=F32)
            r = r + lax.dot_general(q[m], e_ref[m, :, cols(c)], NT, preferred_element_type=F32)
            acc[m] = acc[m] + r
    for m in range(MATS):
        p_ref[m * 8 : m * 8 + 8, :] = fold(acc[m])


def first_left(grads, errors, q):
    wide = pltpu.VMEM((MATS, ROWS, COLS), BF16)
    return kernel(
        first_left_kernel, (pltpu.VMEM((16, ROWS), F32), wide, wide), [ANYWHERE] * 3, "first_left",
        [pltpu.VMEM((MATS, RANK, COLS), F32)] + [pltpu.SemaphoreType.DMA((STEPS,))] * 3,
    )(hbm(grads), hbm(errors), hbm(q))


def left_kernel(slot, ks, at, n_q, *refs):
    q_refs, (g_ref, e_ref), acc_ref, o_ref = refs[:n_q], refs[n_q : n_q + 2], refs[n_q + 2 : -1], refs[-1]
    m = matrix(slot)
    acc = acc_ref[0][...] if acc_ref else jnp.zeros((24, ROWS), F32)
    for i, k in enumerate(ks):
        q_ref = q_refs[i if n_q > 1 else 0]
        for h in range(2):
            q = three(block_of(q_ref, k if at else 0, h))
            acc = acc + lax.dot_general(q, g_ref[m, :, half(k, h)], NT, preferred_element_type=F32)
            acc = acc + lax.dot_general(q, e_ref[m, :, half(k, h)], NT, preferred_element_type=F32)
    o_ref[...] = acc


def left_part(slot, ks, parts, g, e, acc=()):
    at = parts[0].shape[0] > DEEP
    return kernel(
        functools.partial(left_kernel, slot, ks, at, len(parts)), pltpu.VMEM((24, ROWS), F32), [IN_VMEM] * (len(parts) + 2 + len(acc)),
        "left_own" if slot == 0 else "left_other", flops=10**9,
    )(*map(vmem, parts), vmem(g), vmem(e), *map(vmem, acc))


def both_kernel(own_ref, other_ref, p_ref):
    p_ref[rows(matrix(0)), :] = fold(own_ref[...])
    p_ref[rows(matrix(1)), :] = fold(other_ref[...])


def left_both(own, other):
    return kernel(both_kernel, pltpu.VMEM((16, ROWS), F32), [IN_VMEM] * 2, "left_both")(vmem(own), vmem(other))


def right_kernel(slot, p0, p1, p2, p3, g_ref, e_ref, o_ref, *mean_ref):
    m = matrix(slot)
    p = ((p0[...] + p1[...]) + (p2[...] + p3[...])) * (1.0 / SIDE)
    if mean_ref:
        mean_ref[0][...] = p
    p = jnp.where(m == 0, p[0:8], p[8:16])
    pieces = three(p)
    gram = lax.dot_general(p, p, NT, precision=lax.Precision.HIGHEST, preferred_element_type=F32)
    gram = jnp.concatenate([gram, jnp.zeros((8, 120), F32)], axis=1)
    for k in range(SIDE):
        o_ref[k, DEEP : DEEP + 8, :] = gram
        for h in range(2):
            s = slice(k * QUARTER + h * BLOCK, k * QUARTER + (h + 1) * BLOCK)
            r = jnp.dot(pieces, g_ref[m, :, s], preferred_element_type=F32)
            r = fold(r + jnp.dot(pieces, e_ref[m, :, s], preferred_element_type=F32))
            for i in range(BLOCK // 128):
                t = h * (BLOCK // 128) + i
                o_ref[k, t * 8 : t * 8 + 8, :] = r[:, i * 128 : (i + 1) * 128]


def right(slot, p_all, g, e, keep=False):
    out = (pltpu.VMEM((SIDE, DEEP + 8, 128), F32),) + ((pltpu.VMEM((16, ROWS), F32),) if keep else ())
    return kernel(
        functools.partial(right_kernel, slot), out, [IN_VMEM] * 6, "right_own" if slot == 0 else "right_other", flops=10**9,
    )(*map(vmem, p_all), vmem(g), vmem(e))


def pick_kernel(mine_ref, arrived_ref, *o_refs):
    for k, o_ref in enumerate(o_refs):
        o_ref[...] = mine_ref[lax.axis_index("x") ^ k] + arrived_ref[lax.axis_index("x") ^ k]


def pick(mine, arrived):
    return kernel(pick_kernel, (pltpu.VMEM((DEEP + 8, 128), F32),) * SIDE, [IN_VMEM] * 2, "pick")(
        vmem(mine), vmem(arrived))


def add_kernel(a, b, c, d, *o_refs):
    total = (a[...] + b[...]) + (c[...] + d[...])
    o_refs[0][...] = total[0 : o_refs[0].shape[0]]
    if len(o_refs) > 1:
        o_refs[1][...] = total[DEEP : DEEP + 8]


def add(parts, *rows):
    return kernel(add_kernel, tuple(pltpu.VMEM((r, 128), F32) for r in rows), [IN_VMEM] * SIDE, "add")(*map(vmem, parts))


def hat_pieces(lower, p):
    one, two, rest = split3(small_dot(lower, p))
    pieces = jnp.concatenate([one, one, two, two, one, rest, jnp.zeros((80, ROWS), F32)], axis=0)
    return jnp.concatenate([pieces, jnp.zeros((128, 64), F32)], axis=1).T.astype(BF16)


def lower_kernel(gram_ref, *refs):
    lower = inverse_lower(gram_ref[...])
    if len(refs) > 1:
        p_ref, o_ref, hat_ref = refs
        hat_ref[...] = hat_pieces(lower, p_ref[rows(matrix(0)), :])
    refs[-2 if len(refs) > 1 else 0][...] = lower


def lower_inverse(gram, p):
    out = (pltpu.VMEM((8, 128), F32),) + ((pltpu.VMEM((256, 128), BF16),) if p else ())
    return kernel(lower_kernel, out, [IN_VMEM] * (1 + len(p)), "lower_inverse", flops=10**9)(vmem(gram), *map(vmem, p))


def normal_kernel(z0, z1, z2, z3, lower_ref, o_ref):
    total = ((z0[...] + z1[...]) + (z2[...] + z3[...])) * (1.0 / SIDE)
    lower = lower_ref[...]
    for t in range(DEEP // 8):
        o_ref[t * 8 : t * 8 + 8, :] = small_dot(lower, total[t * 8 : t * 8 + 8])


def normal(z_all, lower):
    return kernel(normal_kernel, pltpu.VMEM((DEEP, 128), F32), [IN_VMEM] * 5, "normal")(*map(vmem, z_all), vmem(lower))


def join_kernel(q0, q1, q2, q3, lower_ref, o_ref):
    for k, q_ref in enumerate((q0, q1, q2, q3)):
        o_ref[k * DEEP : (k + 1) * DEEP, :] = q_ref[...]
    o_ref[SIDE * DEEP :, :] = lower_ref[...]


def join(parts, lower):
    return kernel(join_kernel, pltpu.VMEM((SIDE * DEEP + 8, 128), F32), [IN_VMEM] * 5, "join")(*map(vmem, parts), vmem(lower))


def final_kernel(slot, ks, n_q, *refs):
    q_refs, (p_ref, g_ref, e_ref), (a_hbm, n_hbm, q_hbm, a_buf, n_buf, q_buf, a_sem, n_sem, q_sem) = refs[:n_q], refs[n_q : n_q + 3], refs[-9:]
    m = matrix(slot)
    copies = []
    hat = p_ref[...] if slot == 0 else hat_pieces(q_refs[0][SIDE * DEEP :, :], p_ref[rows(m), :])
    hat = hat[0:ROWS, 0:48]
    for j, k in enumerate(ks):
        for h in range(2):
            i = j * 2 + h
            s = half(k, h)
            q = block_of(q_refs[j], 0, h) if slot == 0 else block_of(q_refs[0], k, h)
            q_buf[i] = q
            one, two, rest = split3(q)
            pieces = jnp.concatenate([one, two, one, two, rest, one], axis=0).astype(BF16)
            full = jnp.dot(hat, pieces, preferred_element_type=F32)
            a_buf[i] = full.astype(BF16)
            n_buf[i] = (g_ref[m, :, s].astype(F32) + e_ref[m, :, s].astype(F32) - full).astype(BF16)
            copies.append(pltpu.make_async_copy(a_buf.at[i], a_hbm.at[m, :, s], a_sem.at[i]))
            copies.append(pltpu.make_async_copy(n_buf.at[i], n_hbm.at[0, m, :, s], n_sem.at[i]))
            copies.append(pltpu.make_async_copy(q_buf.at[i], q_hbm.at[m, :, s], q_sem.at[i]))
            for copy in copies[-3:]:
                copy.start()
    for copy in copies:
        copy.wait()


def final(slot, ks, parts, p, g, e, before=()):
    n = len(ks) * 2
    n_in = len(parts) + 3
    return pl.pallas_call(
        functools.partial(final_kernel, slot, ks, len(parts)),
        in_specs=[IN_VMEM] * n_in + [ANYWHERE] * len(before),
        out_specs=(ANYWHERE,) * 3,
        out_shape=(jax.ShapeDtypeStruct((MATS, ROWS, COLS), BF16), jax.ShapeDtypeStruct((1, MATS, ROWS, COLS), BF16),
                   jax.ShapeDtypeStruct((MATS, RANK, COLS), F32)),
        scratch_shapes=[pltpu.VMEM((n, ROWS, BLOCK), BF16), pltpu.VMEM((n, ROWS, BLOCK), BF16),
                        pltpu.VMEM((n, RANK, BLOCK), F32)] + [pltpu.SemaphoreType.DMA((n,))] * 3,
        input_output_aliases={n_in + i: i for i in range(len(before))},
        compiler_params=pltpu.CompilerParams(vmem_limit_bytes=16 * 1024 * 1024),
        cost_estimate=pl.CostEstimate(flops=10**9, bytes_accessed=10**6, transcendentals=0),
        name="residual_own" if slot == 0 else "residual_other",
    )(*map(vmem, (*parts, p, g, e)), *before)


def swap(a, axis, k):
    return lax.ppermute(a, axis, [(i, i ^ k) for i in range(lax.axis_size(axis))])


def cross(a, axis, k):
    return lax.ppermute(a, (axis, "core"), [(i * 2 + c, (i ^ k) * 2 + (c ^ (k & 1))) for i in range(SIDE) for c in range(2)])


def everyones(a, axis, move):
    return (a,) + tuple(move(a, axis, k) for k in (1, 2, 3))


def right_sum(p_own, g, e, keep):
    p_all = everyones(p_own, "dp", swap)
    (theirs,) = right(1, p_all, g, e)
    arrived = swap(theirs, "core", 1)
    mine, *p = right(0, p_all, g, e, keep)
    parts = pick(mine, arrived)
    (z,) = add((parts[0],) + tuple(cross(parts[k], "x", k) for k in (1, 2, 3)), DEEP + 8)
    z, gram = add(everyones(z, "y", cross), DEEP, 8)
    z_all = everyones(z, "dp", cross)
    lower, *hat = lower_inverse(gram, p)
    parts = everyones(normal(z_all, lower), "x", cross)
    return parts, lower, p + hat


def after(parts, out):
    q1, q2, out = lax.optimization_barrier((parts[1], parts[2], out))
    return (parts[0], q1, q2, parts[3]), out


def per_device(grads, errors, q_init):
    p_own, g, e = first_left(grads, errors, jnp.swapaxes(q_init, 1, 2))
    parts, lower, _ = right_sum(p_own, g, e, False)
    own = left_part(0, (0,), parts[:1], g, e)
    parts, own = after(parts, left_part(0, (3,), parts[3:], g, e, (own,)))
    q_other = swap(join(parts, lower), "core", 1)
    own = left_part(0, (1, 2), parts[1:3], g, e, (own,))
    p_own = left_both(own, left_part(1, (0, 1, 2, 3), (q_other,), g, e))
    parts, lower, (p, hat) = right_sum(p_own, g, e, True)
    out = final(0, (0,), parts[:1], hat, g, e)
    parts, out = after(parts, final(0, (3,), parts[3:], hat, g, e, out))
    q_other = swap(join(parts, lower), "core", 1)
    out = final(0, (1, 2), parts[1:3], hat, g, e, out)
    approx, errors_next, q_next = final(1, (0, 1, 2, 3), (q_other,), p, g, e, out)
    return approx, errors_next, jnp.swapaxes(q_next, 1, 2)


def solution(mesh):
    fine = Mesh(mesh.devices.reshape(4, 4, 4, 2), ("dp", "x", "y", "core"))
    fsdp = ("x", "y", "core")
    in_specs = (P("dp", None, fsdp, None), P("dp", None, fsdp, None), P())
    out_specs = (P(None, fsdp, None), P("dp", None, fsdp, None), P())
    return jax.shard_map(per_device, mesh=fine, in_specs=in_specs, out_specs=out_specs, check_vma=False)
```

```python
import functools

import jax
import jax.numpy as jnp
from jax import lax
from jax.experimental import pallas as pl
from jax.experimental.pallas import tpu as pltpu
from jax.sharding import Mesh, PartitionSpec as P

F32, BF16 = jnp.float32, jnp.bfloat16
MATS, RANK, ROWS, COLS = 2, 8, 192, 6144
CHUNK = 1024
STEPS = COLS // CHUNK
SIDE = 4
QUARTER = COLS // SIDE
BLOCK = QUARTER // 2
DEEP = QUARTER // 128 * RANK
NT = (((1,), (1,)), ((), ()))
IN_VMEM = pl.BlockSpec(memory_space=pltpu.VMEM)
ANYWHERE = pl.BlockSpec(memory_space=pl.ANY)


def vmem(a):
    return pltpu.with_memory_space_constraint(a, pltpu.VMEM)


def hbm(a):
    return pltpu.with_memory_space_constraint(a, pltpu.HBM)


def kernel(body, out_shape, in_specs, name, scratch=(), limit=16, flops=10**7, aliases=None):
    many = isinstance(out_shape, tuple)
    out_specs = tuple(ANYWHERE if isinstance(s, jax.ShapeDtypeStruct) else IN_VMEM for s in (out_shape if many else (out_shape,)))
    return pl.pallas_call(
        body,
        in_specs=in_specs,
        out_specs=out_specs if many else out_specs[0],
        out_shape=out_shape,
        scratch_shapes=list(scratch),
        input_output_aliases=aliases or {},
        compiler_params=pltpu.CompilerParams(vmem_limit_bytes=limit * 1024 * 1024),
        cost_estimate=pl.CostEstimate(flops=flops, bytes_accessed=10**6, transcendentals=0),
        name=name,
    )


def split3(a):
    one = a.astype(BF16).astype(F32)
    rest = a - one
    two = rest.astype(BF16).astype(F32)
    return one, two, rest - two


def three(a):
    return jnp.concatenate(split3(a), axis=0).astype(BF16)


def fold(r):
    return r[0:8] + r[8:16] + r[16:24]


def small_dot(a, b):
    total = a[:, 0:1] * b[0:1, :]
    for k in range(1, RANK):
        total = total + a[:, k : k + 1] * b[k : k + 1, :]
    return total


def inverse_lower(gram):
    row = lax.broadcasted_iota(jnp.int32, (8, 128), 0)
    lane = lax.broadcasted_iota(jnp.int32, (8, 128), 1)
    a = jnp.where(lane < RANK, gram, jnp.where(lane == row + RANK, 1.0, 0.0).astype(F32))
    for k in range(RANK):
        pivot = a[k : k + 1, k : k + 1]
        inv = lax.rsqrt(pivot)
        inv = inv * (1.5 - 0.5 * pivot * inv * inv)
        top = a[k : k + 1, :] * inv
        below = a - (a[:, k : k + 1] * inv) * top
        a = jnp.where(row == k, top, jnp.where(row > k, below, a))
    return jnp.concatenate([a[:, RANK : 2 * RANK], jnp.zeros((8, 120), F32)], axis=1)


def block_of(q_ref, k, h):
    first = k * DEEP + h * (BLOCK // 128) * 8
    return jnp.concatenate([q_ref[first + i * 8 : first + i * 8 + 8, :] for i in range(BLOCK // 128)], axis=1)


def half(k, h):
    return pl.ds(pl.multiple_of((lax.axis_index("x") ^ k) * QUARTER + h * BLOCK, BLOCK), BLOCK)


def matrix(slot):
    parity = lax.axis_index("x") ^ lax.axis_index("y") ^ lax.axis_index("dp")
    return lax.axis_index("core") ^ (parity & 1) ^ slot


def here():
    return lax.axis_index("core")


def rows(m):
    return pl.ds(pl.multiple_of(m * 8, 8), 8)


def cols(c):
    return slice(c * CHUNK, (c + 1) * CHUNK)


def first_left_kernel(g_hbm, e_hbm, q_hbm, p_ref, g_ref, e_ref, q_ref, g_sem, e_sem, q_sem):
    copies = []
    for c in range(STEPS):
        s = pl.ds(c * CHUNK, CHUNK)
        copies.append((
            pltpu.make_async_copy(q_hbm.at[:, :, s], q_ref.at[:, :, s], q_sem.at[c]),
            pltpu.make_async_copy(g_hbm.at[0, :, :, s], g_ref.at[:, :, s], g_sem.at[c]),
            pltpu.make_async_copy(e_hbm.at[0, :, :, s], e_ref.at[:, :, s], e_sem.at[c]),
        ))
        for copy in copies[c]:
            copy.start()
    acc = [jnp.zeros((24, ROWS), F32)] * MATS
    for c in range(STEPS):
        copies[c][0].wait()
        q = [three(q_ref[m, :, cols(c)]) for m in range(MATS)]
        copies[c][1].wait()
        copies[c][2].wait()
        for m in range(MATS):
            r = lax.dot_general(q[m], g_ref[m, :, cols(c)], NT, preferred_element_type=F32)
            r = r + lax.dot_general(q[m], e_ref[m, :, cols(c)], NT, preferred_element_type=F32)
            acc[m] = acc[m] + r
    for m in range(MATS):
        p_ref[m * 8 : m * 8 + 8, :] = fold(acc[m])


def first_left(grads, errors, q):
    wide = pltpu.VMEM((MATS, ROWS, COLS), BF16)
    return kernel(
        first_left_kernel, (pltpu.VMEM((16, ROWS), F32), wide, wide), [ANYWHERE] * 3, "first_left",
        [pltpu.VMEM((MATS, RANK, COLS), F32)] + [pltpu.SemaphoreType.DMA((STEPS,))] * 3,
    )(hbm(grads), hbm(errors), hbm(q))


def working_kernel(g_ref, e_ref, o_ref):
    m = matrix(1)
    for c in range(STEPS):
        o_ref[:, cols(c)] = g_ref[m, :, cols(c)].astype(F32) + e_ref[m, :, cols(c)].astype(F32)


def working(g, e):
    return kernel(working_kernel, pltpu.VMEM((ROWS, COLS), F32), [IN_VMEM] * 2, "working", flops=10**9)(vmem(g), vmem(e))


def halves_kernel(w_ref, high_ref, low_ref):
    for c in range(STEPS):
        w = w_ref[:, cols(c)]
        high = w.astype(BF16)
        high_ref[:, cols(c)] = high
        low_ref[:, cols(c)] = (w - high.astype(F32)).astype(BF16)


def halves(w):
    out = pltpu.VMEM((ROWS, COLS), BF16)
    return kernel(halves_kernel, (out, out), [IN_VMEM], "halves", flops=10**9)(vmem(w))


def left_kernel(ks, *refs):
    n = len(ks)
    q_refs, (g_ref, e_ref, high_ref, low_ref), acc_ref, o_ref = refs[:n], refs[n : n + 4], refs[n + 4 : -1], refs[-1]
    m = matrix(0)
    acc = [acc_ref[0][i] if acc_ref else jnp.zeros((24, ROWS), F32) for i in range(2)]
    for q_ref, k in zip(q_refs, ks):
        for h in range(2):
            s = half(k, h)
            q = three(block_of(q_ref, 0, h))
            for w in (g_ref[m, :, s], e_ref[m, :, s]):
                acc[0] = acc[0] + lax.dot_general(q, w, NT, preferred_element_type=F32)
            for w in (high_ref[:, s], low_ref[:, s]):
                acc[1] = acc[1] + lax.dot_general(q, w, NT, preferred_element_type=F32)
    if len(o_ref.shape) == 3:
        for i in range(2):
            o_ref[i] = acc[i]
    else:
        for i in range(2):
            o_ref[rows(here() ^ i), :] = fold(acc[i])


def left_part(ks, parts, w, acc=(), last=False):
    out = pltpu.VMEM((16, ROWS) if last else (2, 24, ROWS), F32)
    return kernel(functools.partial(left_kernel, ks), out, [IN_VMEM] * (len(parts) + 4 + len(acc)), "left_factor", flops=10**9)(
        *map(vmem, (*parts, *w, *acc)))


def gram_tile(*ps):
    gram = sum(lax.dot_general(p, p, NT, precision=lax.Precision.HIGHEST, preferred_element_type=F32) for p in ps)
    return jnp.concatenate([gram, jnp.zeros((8, 120), F32)], axis=1)


def mean_of(p0, p1, p2, p3):
    return ((p0[...] + p1[...]) + (p2[...] + p3[...])) * (1.0 / SIDE)


def put_tiles(o_ref, k, h, r):
    for i in range(BLOCK // 128):
        t = (h * (BLOCK // 128) + i) * 8
        o_ref[(slice(t, t + 8),) if k is None else (k, slice(t, t + 8))] = r[:, i * 128 : (i + 1) * 128]


def right_kernel(slot, p0, p1, p2, p3, g_ref, e_ref, o_ref):
    m = matrix(slot)
    p = mean_of(p0, p1, p2, p3)
    p = jnp.where(m == 0, p[0:8], p[8:16])
    pieces = three(p)
    gram = gram_tile(p)
    for k in range(SIDE):
        o_ref[k, DEEP : DEEP + 8, :] = gram
        for h in range(2):
            s = slice(k * QUARTER + h * BLOCK, k * QUARTER + (h + 1) * BLOCK)
            r = jnp.dot(pieces, g_ref[m, :, s], preferred_element_type=F32)
            put_tiles(o_ref, k, h, fold(r + jnp.dot(pieces, e_ref[m, :, s], preferred_element_type=F32)))


def right(slot, p_all, g, e):
    return kernel(
        functools.partial(right_kernel, slot), pltpu.VMEM((SIDE, DEEP + 8, 128), F32), [IN_VMEM] * 6,
        "right_own" if slot == 0 else "right_other", flops=10**9,
    )(*map(vmem, p_all), vmem(g), vmem(e))


def right_both_kernel(ks, p0, p1, p2, p3, g_ref, e_ref, high_ref, low_ref, *o_refs):
    m = matrix(0)
    mean = mean_of(p0, p1, p2, p3)
    if len(o_refs) > len(ks):
        o_refs[-1][...] = mean
    mine, theirs = (jnp.where(core == 0, mean[0:8], mean[8:16]) for core in (here(), here() ^ 1))
    gram = gram_tile(mean[0:8], mean[8:16])
    mine, theirs = three(mine), three(theirs)
    for o_ref, k in zip(o_refs, ks):
        o_ref[DEEP : DEEP + 8, :] = gram
        for h in range(2):
            s = half(k, h)
            r = jnp.dot(mine, g_ref[m, :, s], preferred_element_type=F32) + jnp.dot(mine, e_ref[m, :, s], preferred_element_type=F32)
            r = r + jnp.dot(theirs, high_ref[:, s], preferred_element_type=F32)
            put_tiles(o_ref, None, h, fold(r + jnp.dot(theirs, low_ref[:, s], preferred_element_type=F32)))


def right_both(ks, p_all, w, keep):
    out = (pltpu.VMEM((DEEP + 8, 128), F32),) * len(ks) + ((pltpu.VMEM((16, ROWS), F32),) if keep else ())
    return kernel(functools.partial(right_both_kernel, ks), out, [IN_VMEM] * 8, "right_both", flops=10**9)(*map(vmem, (*p_all, *w)))


def pick_kernel(mine_ref, arrived_ref, _, *o_refs):
    for k, o_ref in enumerate(o_refs[:SIDE]):
        o_ref[...] = mine_ref[lax.axis_index("x") ^ k] + arrived_ref[lax.axis_index("x") ^ k]


def pick(mine, arrived, later):
    out = (pltpu.VMEM((DEEP + 8, 128), F32),) * SIDE + (pltpu.VMEM(later.shape, later.dtype),)
    return kernel(pick_kernel, out, [IN_VMEM] * 3, "pick", aliases={2: SIDE})(vmem(mine), vmem(arrived), vmem(later))


def add_kernel(a, b, c, d, *o_refs):
    total = (a[...] + b[...]) + (c[...] + d[...])
    o_refs[0][...] = total[0 : o_refs[0].shape[0]]
    if len(o_refs) > 1:
        o_refs[1][...] = total[DEEP : DEEP + 8]


def add(parts, *rows):
    return kernel(add_kernel, tuple(pltpu.VMEM((r, 128), F32) for r in rows), [IN_VMEM] * SIDE, "add")(*map(vmem, parts))


def hat_pieces(lower, p):
    one, two, rest = split3(small_dot(lower, p))
    pieces = jnp.concatenate([one, one, two, two, one, rest, jnp.zeros((80, ROWS), F32)], axis=0)
    return jnp.concatenate([pieces, jnp.zeros((128, 64), F32)], axis=1).T.astype(BF16)


def lower_kernel(gram_ref, *refs):
    lower = inverse_lower(gram_ref[...])
    if len(refs) > 1:
        p_ref, o_ref, hat_ref = refs
        hat_ref[...] = hat_pieces(lower, p_ref[rows(here()), :])
    refs[-2 if len(refs) > 1 else 0][...] = lower


def lower_inverse(gram, p):
    out = (pltpu.VMEM((8, 128), F32),) + ((pltpu.VMEM((256, 128), BF16),) if p else ())
    return kernel(lower_kernel, out, [IN_VMEM] * (1 + len(p)), "lower_inverse", flops=10**9)(vmem(gram), *map(vmem, p))


def normal_kernel(z0, z1, z2, z3, lower_ref, o_ref):
    total = ((z0[...] + z1[...]) + (z2[...] + z3[...])) * (1.0 / SIDE)
    lower = lower_ref[...]
    for t in range(DEEP // 8):
        o_ref[t * 8 : t * 8 + 8, :] = small_dot(lower, total[t * 8 : t * 8 + 8])


def normal(z_all, lower):
    return kernel(normal_kernel, pltpu.VMEM((DEEP, 128), F32), [IN_VMEM] * 5, "normal")(*map(vmem, z_all), vmem(lower))


def join_kernel(q0, q1, q2, q3, lower_ref, p_ref, o_ref):
    for k, q_ref in enumerate((q0, q1, q2, q3)):
        o_ref[k * DEEP : (k + 1) * DEEP, :] = q_ref[...]
    first = SIDE * DEEP
    o_ref[first : first + 8, :] = lower_ref[...]
    p = p_ref[rows(here() ^ 1), :]
    o_ref[first + 8 : first + 16, :] = p[:, 0:128]
    o_ref[first + 16 : first + 24, :] = jnp.concatenate([p[:, 128:ROWS], jnp.zeros((8, 256 - ROWS), F32)], axis=1)


def join(parts, lower, p):
    return kernel(join_kernel, pltpu.VMEM((SIDE * DEEP + 24, 128), F32), [IN_VMEM] * 6, "join")(*map(vmem, (*parts, lower, p)))


def final_kernel(slot, ks, n_q, n_in, *refs):
    q_refs, hat_ref, (g_ref, e_ref) = refs[:n_q], refs[n_q:n_in], refs[n_in : n_in + 2]
    a_hbm, n_hbm, q_hbm, a_buf, n_buf, q_buf, a_sem, n_sem, q_sem = refs[-9:]
    m = matrix(slot)
    copies = []
    if hat_ref:
        hat = hat_ref[0][...]
    else:
        lower, p = q_refs[0][SIDE * DEEP : SIDE * DEEP + 8, :], q_refs[0][SIDE * DEEP + 8 :, :]
        hat = hat_pieces(lower, jnp.concatenate([p[0:8], p[8:16, 0 : ROWS - 128]], axis=1))
    hat = hat[0:ROWS, 0:48]
    for j, k in enumerate(ks):
        for h in range(2):
            i = j * 2 + h
            s = half(k, h)
            q = block_of(q_refs[j], 0, h) if slot == 0 else block_of(q_refs[0], k, h)
            q_buf[i] = q
            one, two, rest = split3(q)
            pieces = jnp.concatenate([one, two, one, two, rest, one], axis=0).astype(BF16)
            full = jnp.dot(hat, pieces, preferred_element_type=F32)
            a_buf[i] = full.astype(BF16)
            n_buf[i] = (g_ref[m, :, s].astype(F32) + e_ref[m, :, s].astype(F32) - full).astype(BF16)
            copies.append(pltpu.make_async_copy(a_buf.at[i], a_hbm.at[m, :, s], a_sem.at[i]))
            copies.append(pltpu.make_async_copy(n_buf.at[i], n_hbm.at[0, m, :, s], n_sem.at[i]))
            copies.append(pltpu.make_async_copy(q_buf.at[i], q_hbm.at[m, :, s], q_sem.at[i]))
            for copy in copies[-3:]:
                copy.start()
    for copy in copies:
        copy.wait()


def final(slot, ks, parts, hat, g, e, before=()):
    n = len(ks) * 2
    n_in = len(parts) + len(hat)
    return pl.pallas_call(
        functools.partial(final_kernel, slot, ks, len(parts), n_in),
        in_specs=[IN_VMEM] * (n_in + 2) + [ANYWHERE] * len(before),
        out_specs=(ANYWHERE,) * 3,
        out_shape=(jax.ShapeDtypeStruct((MATS, ROWS, COLS), BF16), jax.ShapeDtypeStruct((1, MATS, ROWS, COLS), BF16),
                   jax.ShapeDtypeStruct((MATS, RANK, COLS), F32)),
        scratch_shapes=[pltpu.VMEM((n, ROWS, BLOCK), BF16), pltpu.VMEM((n, ROWS, BLOCK), BF16),
                        pltpu.VMEM((n, RANK, BLOCK), F32)] + [pltpu.SemaphoreType.DMA((n,))] * 3,
        input_output_aliases={n_in + 2 + i: i for i in range(len(before))},
        compiler_params=pltpu.CompilerParams(vmem_limit_bytes=16 * 1024 * 1024),
        cost_estimate=pl.CostEstimate(flops=10**9, bytes_accessed=10**6, transcendentals=0),
        name="residual_own" if slot == 0 else "residual_other",
    )(*map(vmem, (*parts, *hat, g, e)), *before)


def swap(a, axis, k):
    return lax.ppermute(a, axis, [(i, i ^ k) for i in range(lax.axis_size(axis))])


def cross(a, axis, k):
    return lax.ppermute(a, (axis, "core"), [(i * 2 + c, (i ^ k) * 2 + (c ^ (k & 1))) for i in range(SIDE) for c in range(2)])


def everyones(a, axis, move, order=(1, 2, 3)):
    moved = {k: move(a, axis, k) for k in order}
    return (a, moved[1], moved[2], moved[3])


def right_sum(parts, p=()):
    (z,) = add(parts[:1] + tuple(cross(parts[k], "x", k) for k in (1, 2, 3)), DEEP + 8)
    z, gram = add(everyones(z, "y", cross), DEEP, 8)
    z_all = everyones(z, "dp", cross)
    lower, *hat = lower_inverse(gram, p)
    return everyones(normal(z_all, lower), "x", cross, (2, 1, 3)), lower, hat


def after(parts, out, *ks):
    *late, out = lax.optimization_barrier(tuple(parts[k] for k in ks) + (out,))
    return tuple(late[ks.index(k)] if k in ks else parts[k] for k in range(SIDE)), out


def per_device(grads, errors, q_init):
    p, g, e = first_left(grads, errors, jnp.swapaxes(q_init, 1, 2))
    p_all = everyones(p, "dp", swap)
    arrived = swap(right(1, p_all, g, e), "core", 1)
    *parts, w = pick(right(0, p_all, g, e), arrived, working(g, e))
    w = (g, e) + tuple(halves(swap(w, "core", 1)))
    parts, _, _ = right_sum(tuple(parts))

    acc = left_part((0,), parts[:1], w)
    parts, acc = after(parts, left_part((3,), parts[3:], w, (acc,)), 1)
    acc = left_part((1,), parts[1:2], w, (acc,))
    p_all = everyones(left_part((2,), parts[2:3], w, (acc,), True), "dp", cross)
    z2, z3, p = right_both((2, 3), p_all, w, True)
    z1, z0 = right_both((1, 0), p_all, w, False)
    parts, lower, hat = right_sum((z0, z1, z2, z3), (p,))

    out = final(0, (0,), parts[:1], hat, g, e)
    parts, out = after(parts, final(0, (3,), parts[3:], hat, g, e, out), 1, 2)
    other = swap(join(parts, lower, p), "core", 1)
    out = final(0, (1, 2), parts[1:3], hat, g, e, out)
    approx, errors_next, q_next = final(1, (0, 1, 2, 3), (other,), (), g, e, out)
    return approx, errors_next, jnp.swapaxes(q_next, 1, 2)


def solution(mesh):
    fine = Mesh(mesh.devices.reshape(4, 4, 4, 2), ("dp", "x", "y", "core"))
    fsdp = ("x", "y", "core")
    in_specs = (P("dp", None, fsdp, None), P("dp", None, fsdp, None), P())
    out_specs = (P(None, fsdp, None), P("dp", None, fsdp, None), P())
    return jax.shard_map(per_device, mesh=fine, in_specs=in_specs, out_specs=out_specs, check_vma=False)
```

```python
import functools

import jax
import jax.numpy as jnp
from jax import lax
from jax.experimental import pallas as pl
from jax.experimental.pallas import tpu as pltpu
from jax.sharding import Mesh, PartitionSpec as P

F32, BF16 = jnp.float32, jnp.bfloat16
MATS, RANK, ROWS, COLS = 2, 8, 192, 6144
CHUNK = 1024
STEPS = COLS // CHUNK
SIDE = 4
QUARTER = COLS // SIDE
BLOCK = QUARTER // 2
DEEP = QUARTER // 128 * RANK
NT = (((1,), (1,)), ((), ()))
IN_VMEM = pl.BlockSpec(memory_space=pltpu.VMEM)
ANYWHERE = pl.BlockSpec(memory_space=pl.ANY)


def vmem(a):
    return pltpu.with_memory_space_constraint(a, pltpu.VMEM)


def hbm(a):
    return pltpu.with_memory_space_constraint(a, pltpu.HBM)


def kernel(body, out_shape, in_specs, name, scratch=(), limit=16, flops=10**7, aliases=None):
    many = isinstance(out_shape, tuple)
    out_specs = tuple(ANYWHERE if isinstance(s, jax.ShapeDtypeStruct) else IN_VMEM for s in (out_shape if many else (out_shape,)))
    return pl.pallas_call(
        body,
        in_specs=in_specs,
        out_specs=out_specs if many else out_specs[0],
        out_shape=out_shape,
        scratch_shapes=list(scratch),
        input_output_aliases=aliases or {},
        compiler_params=pltpu.CompilerParams(vmem_limit_bytes=limit * 1024 * 1024),
        cost_estimate=pl.CostEstimate(flops=flops, bytes_accessed=10**6, transcendentals=0),
        name=name,
    )


def split3(a):
    one = a.astype(BF16).astype(F32)
    rest = a - one
    two = rest.astype(BF16).astype(F32)
    return one, two, rest - two


def three(a):
    return jnp.concatenate(split3(a), axis=0).astype(BF16)


def fold(r):
    return r[0:8] + r[8:16] + r[16:24]


def small_dot(a, b):
    total = a[:, 0:1] * b[0:1, :]
    for k in range(1, RANK):
        total = total + a[:, k : k + 1] * b[k : k + 1, :]
    return total


def inverse_lower(gram):
    row = lax.broadcasted_iota(jnp.int32, (8, 128), 0)
    lane = lax.broadcasted_iota(jnp.int32, (8, 128), 1)
    a = jnp.where(lane < RANK, gram, jnp.where(lane == row + RANK, 1.0, 0.0).astype(F32))
    for k in range(RANK):
        pivot = a[k : k + 1, k : k + 1]
        inv = lax.rsqrt(pivot)
        inv = inv * (1.5 - 0.5 * pivot * inv * inv)
        top = a[k : k + 1, :] * inv
        below = a - (a[:, k : k + 1] * inv) * top
        a = jnp.where(row == k, top, jnp.where(row > k, below, a))
    return jnp.concatenate([a[:, RANK : 2 * RANK], jnp.zeros((8, 120), F32)], axis=1)


def block_of(q_ref, k, h):
    first = k * DEEP + h * (BLOCK // 128) * 8
    return jnp.concatenate([q_ref[first + i * 8 : first + i * 8 + 8, :] for i in range(BLOCK // 128)], axis=1)


def half(k, h):
    return pl.ds(pl.multiple_of((lax.axis_index("x") ^ k) * QUARTER + h * BLOCK, BLOCK), BLOCK)


def matrix(slot):
    parity = lax.axis_index("x") ^ lax.axis_index("y") ^ lax.axis_index("dp")
    return lax.axis_index("core") ^ (parity & 1) ^ slot


def here():
    return lax.axis_index("core")


def rows(m):
    return pl.ds(pl.multiple_of(m * 8, 8), 8)


def cols(c):
    return slice(c * CHUNK, (c + 1) * CHUNK)


def first_left_kernel(g_hbm, e_hbm, q_hbm, p_ref, g_ref, e_ref, q_ref, g_sem, e_sem, q_sem):
    copies = []
    for c in range(STEPS):
        s = pl.ds(c * CHUNK, CHUNK)
        copies.append((
            pltpu.make_async_copy(q_hbm.at[:, :, s], q_ref.at[:, :, s], q_sem.at[c]),
            pltpu.make_async_copy(g_hbm.at[0, :, :, s], g_ref.at[:, :, s], g_sem.at[c]),
            pltpu.make_async_copy(e_hbm.at[0, :, :, s], e_ref.at[:, :, s], e_sem.at[c]),
        ))
        for copy in copies[c]:
            copy.start()
    acc = [jnp.zeros((24, ROWS), F32)] * MATS
    for c in range(STEPS):
        copies[c][0].wait()
        q = [three(q_ref[m, :, cols(c)]) for m in range(MATS)]
        copies[c][1].wait()
        copies[c][2].wait()
        for m in range(MATS):
            r = lax.dot_general(q[m], g_ref[m, :, cols(c)], NT, preferred_element_type=F32)
            r = r + lax.dot_general(q[m], e_ref[m, :, cols(c)], NT, preferred_element_type=F32)
            acc[m] = acc[m] + r
    for m in range(MATS):
        p_ref[m * 8 : m * 8 + 8, :] = fold(acc[m])


def first_left(grads, errors, q):
    wide = pltpu.VMEM((MATS, ROWS, COLS), BF16)
    return kernel(
        first_left_kernel, (pltpu.VMEM((16, ROWS), F32), wide, wide), [ANYWHERE] * 3, "first_left",
        [pltpu.VMEM((MATS, RANK, COLS), F32)] + [pltpu.SemaphoreType.DMA((STEPS,))] * 3,
    )(hbm(grads), hbm(errors), hbm(q))


def working_kernel(g_ref, e_ref, o_ref):
    m = matrix(1)
    for c in range(STEPS):
        o_ref[:, cols(c)] = g_ref[m, :, cols(c)].astype(F32) + e_ref[m, :, cols(c)].astype(F32)


def working(g, e):
    return kernel(working_kernel, pltpu.VMEM((ROWS, COLS), F32), [IN_VMEM] * 2, "working", flops=10**9)(vmem(g), vmem(e))


def halves_kernel(w_ref, high_ref, low_ref):
    for c in range(STEPS):
        w = w_ref[:, cols(c)]
        high = w.astype(BF16)
        high_ref[:, cols(c)] = high
        low_ref[:, cols(c)] = (w - high.astype(F32)).astype(BF16)


def halves(w):
    out = pltpu.VMEM((ROWS, COLS), BF16)
    return kernel(halves_kernel, (out, out), [IN_VMEM], "halves", flops=10**9)(vmem(w))


def left_kernel(ks, *refs):
    n = len(ks)
    q_refs, (g_ref, e_ref, high_ref, low_ref), acc_ref, o_ref = refs[:n], refs[n : n + 4], refs[n + 4 : -1], refs[-1]
    m = matrix(0)
    acc = [acc_ref[0][i] if acc_ref else jnp.zeros((24, ROWS), F32) for i in range(2)]
    for q_ref, k in zip(q_refs, ks):
        for h in range(2):
            s = half(k, h)
            q = three(block_of(q_ref, 0, h))
            for w in (g_ref[m, :, s], e_ref[m, :, s]):
                acc[0] = acc[0] + lax.dot_general(q, w, NT, preferred_element_type=F32)
            for w in (high_ref[:, s], low_ref[:, s]):
                acc[1] = acc[1] + lax.dot_general(q, w, NT, preferred_element_type=F32)
    if len(o_ref.shape) == 3:
        for i in range(2):
            o_ref[i] = acc[i]
    else:
        for i in range(2):
            o_ref[rows(here() ^ i), :] = fold(acc[i])


def left_part(ks, parts, w, acc=(), last=False):
    out = pltpu.VMEM((16, ROWS) if last else (2, 24, ROWS), F32)
    return kernel(functools.partial(left_kernel, ks), out, [IN_VMEM] * (len(parts) + 4 + len(acc)), "left_factor", flops=10**9)(
        *map(vmem, (*parts, *w, *acc)))


def gram_tile(*ps):
    gram = sum(lax.dot_general(p, p, NT, precision=lax.Precision.HIGHEST, preferred_element_type=F32) for p in ps)
    return jnp.concatenate([gram, jnp.zeros((8, 120), F32)], axis=1)


def mean_of(p0, p1, p2, p3):
    return ((p0[...] + p1[...]) + (p2[...] + p3[...])) * (1.0 / SIDE)


def put_tiles(o_ref, k, h, r):
    for i in range(BLOCK // 128):
        t = (h * (BLOCK // 128) + i) * 8
        o_ref[(slice(t, t + 8),) if k is None else (k, slice(t, t + 8))] = r[:, i * 128 : (i + 1) * 128]


def right_kernel(slot, p0, p1, p2, p3, g_ref, e_ref, o_ref):
    m = matrix(slot)
    p = mean_of(p0, p1, p2, p3)
    p = jnp.where(m == 0, p[0:8], p[8:16])
    pieces = three(p)
    gram = gram_tile(p)
    for k in range(SIDE):
        o_ref[k, DEEP : DEEP + 8, :] = gram
        for h in range(2):
            s = slice(k * QUARTER + h * BLOCK, k * QUARTER + (h + 1) * BLOCK)
            r = jnp.dot(pieces, g_ref[m, :, s], preferred_element_type=F32)
            put_tiles(o_ref, k, h, fold(r + jnp.dot(pieces, e_ref[m, :, s], preferred_element_type=F32)))


def right(slot, p_all, g, e):
    return kernel(
        functools.partial(right_kernel, slot), pltpu.VMEM((SIDE, DEEP + 8, 128), F32), [IN_VMEM] * 6,
        "right_own" if slot == 0 else "right_other", flops=10**9,
    )(*map(vmem, p_all), vmem(g), vmem(e))


def right_both_kernel(ks, p0, p1, p2, p3, g_ref, e_ref, high_ref, low_ref, *o_refs):
    m = matrix(0)
    mean = mean_of(p0, p1, p2, p3)
    if len(o_refs) > len(ks):
        o_refs[-1][...] = mean
    mine, theirs = (jnp.where(core == 0, mean[0:8], mean[8:16]) for core in (here(), here() ^ 1))
    gram = gram_tile(mean[0:8], mean[8:16])
    mine, theirs = three(mine), three(theirs)
    for o_ref, k in zip(o_refs, ks):
        o_ref[DEEP : DEEP + 8, :] = gram
        for h in range(2):
            s = half(k, h)
            r = jnp.dot(mine, g_ref[m, :, s], preferred_element_type=F32) + jnp.dot(mine, e_ref[m, :, s], preferred_element_type=F32)
            r = r + jnp.dot(theirs, high_ref[:, s], preferred_element_type=F32)
            put_tiles(o_ref, None, h, fold(r + jnp.dot(theirs, low_ref[:, s], preferred_element_type=F32)))


def right_both(ks, p_all, w, keep):
    out = (pltpu.VMEM((DEEP + 8, 128), F32),) * len(ks) + ((pltpu.VMEM((16, ROWS), F32),) if keep else ())
    return kernel(functools.partial(right_both_kernel, ks), out, [IN_VMEM] * 8, "right_both", flops=10**9)(*map(vmem, (*p_all, *w)))


def pick_kernel(mine_ref, arrived_ref, _, *o_refs):
    for k, o_ref in enumerate(o_refs[:SIDE]):
        o_ref[...] = mine_ref[lax.axis_index("x") ^ k] + arrived_ref[lax.axis_index("x") ^ k]


def pick(mine, arrived, later):
    out = (pltpu.VMEM((DEEP + 8, 128), F32),) * SIDE + (pltpu.VMEM(later.shape, later.dtype),)
    return kernel(pick_kernel, out, [IN_VMEM] * 3, "pick", aliases={2: SIDE})(vmem(mine), vmem(arrived), vmem(later))


def add_kernel(a, b, c, d, *o_refs):
    total = (a[...] + b[...]) + (c[...] + d[...])
    o_refs[0][...] = total[0 : o_refs[0].shape[0]]
    if len(o_refs) > 1:
        o_refs[1][...] = total[DEEP : DEEP + 8]


def add(parts, *rows):
    return kernel(add_kernel, tuple(pltpu.VMEM((r, 128), F32) for r in rows), [IN_VMEM] * SIDE, "add")(*map(vmem, parts))


def hat_pieces(lower, p):
    one, two, rest = split3(small_dot(lower, p))
    pieces = jnp.concatenate([one, one, two, two, one, rest, jnp.zeros((80, ROWS), F32)], axis=0)
    return jnp.concatenate([pieces, jnp.zeros((128, 64), F32)], axis=1).T.astype(BF16)


def lower_kernel(gram_ref, *refs):
    lower = inverse_lower(gram_ref[...])
    if len(refs) > 1:
        p_ref, o_ref, hat_ref = refs
        hat_ref[...] = hat_pieces(lower, p_ref[rows(here()), :])
    refs[-2 if len(refs) > 1 else 0][...] = lower


def lower_inverse(gram, p):
    out = (pltpu.VMEM((8, 128), F32),) + ((pltpu.VMEM((256, 128), BF16),) if p else ())
    return kernel(lower_kernel, out, [IN_VMEM] * (1 + len(p)), "lower_inverse", flops=10**9)(vmem(gram), *map(vmem, p))


def normal_kernel(z0, z1, z2, z3, lower_ref, *refs):
    o_ref = refs[-1]
    total = ((z0[...] + z1[...]) + (z2[...] + z3[...])) * (1.0 / SIDE)
    lower = lower_ref[...]
    for t in range(DEEP // 8):
        o_ref[t * 8 : t * 8 + 8, :] = small_dot(lower, total[t * 8 : t * 8 + 8])


def normal(z_all, lower, first):
    return kernel(normal_kernel, pltpu.VMEM((DEEP, 128), F32), [IN_VMEM] * (5 + len(first)), "normal")(*map(vmem, (*z_all, lower, *first)))


def join_kernel(q0, q1, q2, q3, lower_ref, p_ref, o_ref):
    for k, q_ref in enumerate((q0, q1, q2, q3)):
        o_ref[k * DEEP : (k + 1) * DEEP, :] = q_ref[...]
    first = SIDE * DEEP
    o_ref[first : first + 8, :] = lower_ref[...]
    p = p_ref[rows(here() ^ 1), :]
    o_ref[first + 8 : first + 16, :] = p[:, 0:128]
    o_ref[first + 16 : first + 24, :] = jnp.concatenate([p[:, 128:ROWS], jnp.zeros((8, 256 - ROWS), F32)], axis=1)


def join(parts, lower, p):
    return kernel(join_kernel, pltpu.VMEM((SIDE * DEEP + 24, 128), F32), [IN_VMEM] * 6, "join")(*map(vmem, (*parts, lower, p)))


def final_kernel(slot, ks, n_q, n_in, *refs):
    q_refs, hat_ref, (g_ref, e_ref) = refs[:n_q], refs[n_q:n_in], refs[n_in : n_in + 2]
    a_hbm, n_hbm, q_hbm, a_buf, n_buf, q_buf, a_sem, n_sem, q_sem = refs[-9:]
    m = matrix(slot)
    copies = []
    if hat_ref:
        hat = hat_ref[0][...]
    else:
        lower, p = q_refs[0][SIDE * DEEP : SIDE * DEEP + 8, :], q_refs[0][SIDE * DEEP + 8 :, :]
        hat = hat_pieces(lower, jnp.concatenate([p[0:8], p[8:16, 0 : ROWS - 128]], axis=1))
    hat = hat[0:ROWS, 0:48]
    for j, k in enumerate(ks):
        for h in range(2):
            i = j * 2 + h
            s = half(k, h)
            q = block_of(q_refs[j], 0, h) if slot == 0 else block_of(q_refs[0], k, h)
            q_buf[i] = q
            one, two, rest = split3(q)
            pieces = jnp.concatenate([one, two, one, two, rest, one], axis=0).astype(BF16)
            full = jnp.dot(hat, pieces, preferred_element_type=F32)
            a_buf[i] = full.astype(BF16)
            n_buf[i] = (g_ref[m, :, s].astype(F32) + e_ref[m, :, s].astype(F32) - full).astype(BF16)
            copies.append(pltpu.make_async_copy(a_buf.at[i], a_hbm.at[m, :, s], a_sem.at[i]))
            copies.append(pltpu.make_async_copy(n_buf.at[i], n_hbm.at[0, m, :, s], n_sem.at[i]))
            copies.append(pltpu.make_async_copy(q_buf.at[i], q_hbm.at[m, :, s], q_sem.at[i]))
            for copy in copies[-3:]:
                copy.start()
    for copy in copies:
        copy.wait()


def final(slot, ks, parts, hat, g, e, before=()):
    n = len(ks) * 2
    n_in = len(parts) + len(hat)
    return pl.pallas_call(
        functools.partial(final_kernel, slot, ks, len(parts), n_in),
        in_specs=[IN_VMEM] * (n_in + 2) + [ANYWHERE] * len(before),
        out_specs=(ANYWHERE,) * 3,
        out_shape=(jax.ShapeDtypeStruct((MATS, ROWS, COLS), BF16), jax.ShapeDtypeStruct((1, MATS, ROWS, COLS), BF16),
                   jax.ShapeDtypeStruct((MATS, RANK, COLS), F32)),
        scratch_shapes=[pltpu.VMEM((n, ROWS, BLOCK), BF16), pltpu.VMEM((n, ROWS, BLOCK), BF16),
                        pltpu.VMEM((n, RANK, BLOCK), F32)] + [pltpu.SemaphoreType.DMA((n,))] * 3,
        input_output_aliases={n_in + 2 + i: i for i in range(len(before))},
        compiler_params=pltpu.CompilerParams(vmem_limit_bytes=16 * 1024 * 1024),
        cost_estimate=pl.CostEstimate(flops=10**9, bytes_accessed=10**6, transcendentals=0),
        name="residual_own" if slot == 0 else "residual_other",
    )(*map(vmem, (*parts, *hat, g, e)), *before)


def swap(a, axis, k):
    return lax.ppermute(a, axis, [(i, i ^ k) for i in range(lax.axis_size(axis))])


def cross(a, axis, k):
    return lax.ppermute(a, (axis, "core"), [(i * 2 + c, (i ^ k) * 2 + (c ^ (k & 1))) for i in range(SIDE) for c in range(2)])


def everyones(a, axis, move, order=(1, 2, 3)):
    moved = {k: move(a, axis, k) for k in order}
    return (a, moved[1], moved[2], moved[3])


def right_sum(parts, p=(), first=()):
    (z,) = add(parts[:1] + tuple(cross(parts[k], "x", k) for k in (1, 2, 3)), DEEP + 8)
    z, gram = add(everyones(z, "y", cross), DEEP, 8)
    z_all = everyones(z, "dp", cross)
    lower, *hat = lower_inverse(gram, p)
    return everyones(normal(z_all, lower, first), "x", cross, (2, 1, 3)), lower, hat


def after(parts, out, *ks):
    *late, out = lax.optimization_barrier(tuple(parts[k] for k in ks) + (out,))
    return tuple(late[ks.index(k)] if k in ks else parts[k] for k in range(SIDE)), out


def per_device(grads, errors, q_init):
    p, g, e = first_left(grads, errors, jnp.swapaxes(q_init, 1, 2))
    p_all = everyones(p, "dp", swap)
    arrived = swap(right(1, p_all, g, e), "core", 1)
    *parts, w = pick(right(0, p_all, g, e), arrived, working(g, e))
    w = (g, e) + tuple(halves(swap(w, "core", 1)))
    parts, _, _ = right_sum(tuple(parts), first=w[2:])

    acc = left_part((0,), parts[:1], w)
    parts, acc = after(parts, left_part((3,), parts[3:], w, (acc,)), 1)
    acc = left_part((1,), parts[1:2], w, (acc,))
    p_all = everyones(left_part((2,), parts[2:3], w, (acc,), True), "dp", cross)
    z2, z3, p = right_both((2, 3), p_all, w, True)
    z1, z0 = right_both((1, 0), p_all, w, False)
    parts, lower, hat = right_sum((z0, z1, z2, z3), (p,))

    out = final(0, (0,), parts[:1], hat, g, e)
    parts, out = after(parts, final(0, (3,), parts[3:], hat, g, e, out), 1, 2)
    other = swap(join(parts, lower, p), "core", 1)
    out = final(0, (1, 2), parts[1:3], hat, g, e, out)
    approx, errors_next, q_next = final(1, (0, 1, 2, 3), (other,), (), g, e, out)
    return approx, errors_next, jnp.swapaxes(q_next, 1, 2)


def solution(mesh):
    fine = Mesh(mesh.devices.reshape(4, 4, 4, 2), ("dp", "x", "y", "core"))
    fsdp = ("x", "y", "core")
    in_specs = (P("dp", None, fsdp, None), P("dp", None, fsdp, None), P())
    out_specs = (P(None, fsdp, None), P("dp", None, fsdp, None), P())
    return jax.shard_map(per_device, mesh=fine, in_specs=in_specs, out_specs=out_specs, check_vma=False)
```

```python
import functools

import jax
import jax.numpy as jnp
from jax import lax
from jax.experimental import pallas as pl
from jax.experimental.pallas import tpu as pltpu
from jax.sharding import Mesh, PartitionSpec as P

F32, BF16 = jnp.float32, jnp.bfloat16
MATS, RANK, ROWS, COLS = 2, 8, 192, 6144
CHUNK = 1024
STEPS = COLS // CHUNK
SIDE = 4
QUARTER = COLS // SIDE
BLOCK = QUARTER // 2
DEEP = QUARTER // 128 * RANK
NT = (((1,), (1,)), ((), ()))
IN_VMEM = pl.BlockSpec(memory_space=pltpu.VMEM)
ANYWHERE = pl.BlockSpec(memory_space=pl.ANY)


def vmem(a):
    return pltpu.with_memory_space_constraint(a, pltpu.VMEM)


def hbm(a):
    return pltpu.with_memory_space_constraint(a, pltpu.HBM)


def kernel(body, out_shape, in_specs, name, scratch=(), limit=16, flops=10**7, aliases=None):
    many = isinstance(out_shape, tuple)
    out_specs = tuple(ANYWHERE if isinstance(s, jax.ShapeDtypeStruct) else IN_VMEM for s in (out_shape if many else (out_shape,)))
    return pl.pallas_call(
        body,
        in_specs=in_specs,
        out_specs=out_specs if many else out_specs[0],
        out_shape=out_shape,
        scratch_shapes=list(scratch),
        input_output_aliases=aliases or {},
        compiler_params=pltpu.CompilerParams(vmem_limit_bytes=limit * 1024 * 1024),
        cost_estimate=pl.CostEstimate(flops=flops, bytes_accessed=10**6, transcendentals=0),
        name=name,
    )


def split3(a):
    one = a.astype(BF16).astype(F32)
    rest = a - one
    two = rest.astype(BF16).astype(F32)
    return one, two, rest - two


def three(a):
    return jnp.concatenate(split3(a), axis=0).astype(BF16)


def fold(r):
    return r[0:8] + r[8:16] + r[16:24]


def small_dot(a, b):
    total = a[:, 0:1] * b[0:1, :]
    for k in range(1, RANK):
        total = total + a[:, k : k + 1] * b[k : k + 1, :]
    return total


def inverse_lower(gram):
    row = lax.broadcasted_iota(jnp.int32, (8, 128), 0)
    lane = lax.broadcasted_iota(jnp.int32, (8, 128), 1)
    a = jnp.where(lane < RANK, gram, jnp.where(lane == row + RANK, 1.0, 0.0).astype(F32))
    for k in range(RANK):
        pivot = a[k : k + 1, k : k + 1]
        inv = lax.rsqrt(pivot)
        inv = inv * (1.5 - 0.5 * pivot * inv * inv)
        top = a[k : k + 1, :] * inv
        below = a - (a[:, k : k + 1] * inv) * top
        a = jnp.where(row == k, top, jnp.where(row > k, below, a))
    return jnp.concatenate([a[:, RANK : 2 * RANK], jnp.zeros((8, 120), F32)], axis=1)


def block_of(q_ref, k, h):
    first = k * DEEP + h * (BLOCK // 128) * 8
    return jnp.concatenate([q_ref[first + i * 8 : first + i * 8 + 8, :] for i in range(BLOCK // 128)], axis=1)


def half(k, h):
    return pl.ds(pl.multiple_of((lax.axis_index("x") ^ k) * QUARTER + h * BLOCK, BLOCK), BLOCK)


def matrix(slot):
    parity = lax.axis_index("x") ^ lax.axis_index("y") ^ lax.axis_index("dp")
    return lax.axis_index("core") ^ (parity & 1) ^ slot


def here():
    return lax.axis_index("core")


def rows(m):
    return pl.ds(pl.multiple_of(m * 8, 8), 8)


def cols(c):
    return slice(c * CHUNK, (c + 1) * CHUNK)


def first_left_kernel(g_hbm, e_hbm, q_hbm, p_ref, g_ref, e_ref, q_ref, g_sem, e_sem, q_sem):
    copies = []
    for c in range(STEPS):
        s = pl.ds(c * CHUNK, CHUNK)
        copies.append((
            pltpu.make_async_copy(q_hbm.at[:, :, s], q_ref.at[:, :, s], q_sem.at[c]),
            pltpu.make_async_copy(g_hbm.at[0, :, :, s], g_ref.at[:, :, s], g_sem.at[c]),
            pltpu.make_async_copy(e_hbm.at[0, :, :, s], e_ref.at[:, :, s], e_sem.at[c]),
        ))
        for copy in copies[c]:
            copy.start()
    acc = [jnp.zeros((24, ROWS), F32)] * MATS
    for c in range(STEPS):
        copies[c][0].wait()
        q = [three(q_ref[m, :, cols(c)]) for m in range(MATS)]
        copies[c][1].wait()
        copies[c][2].wait()
        for m in range(MATS):
            r = lax.dot_general(q[m], g_ref[m, :, cols(c)], NT, preferred_element_type=F32)
            r = r + lax.dot_general(q[m], e_ref[m, :, cols(c)], NT, preferred_element_type=F32)
            acc[m] = acc[m] + r
    for m in range(MATS):
        p_ref[m * 8 : m * 8 + 8, :] = fold(acc[m])


def first_left(grads, errors, q):
    wide = pltpu.VMEM((MATS, ROWS, COLS), BF16)
    return kernel(
        first_left_kernel, (pltpu.VMEM((16, ROWS), F32), wide, wide), [ANYWHERE] * 3, "first_left",
        [pltpu.VMEM((MATS, RANK, COLS), F32)] + [pltpu.SemaphoreType.DMA((STEPS,))] * 3,
    )(hbm(grads), hbm(errors), hbm(q))


def working_kernel(g_ref, e_ref, o_ref):
    m = matrix(1)
    for c in range(STEPS):
        o_ref[:, cols(c)] = g_ref[m, :, cols(c)].astype(F32) + e_ref[m, :, cols(c)].astype(F32)


def working(g, e):
    return kernel(working_kernel, pltpu.VMEM((ROWS, COLS), F32), [IN_VMEM] * 2, "working", flops=10**9)(vmem(g), vmem(e))


def halves_kernel(w_ref, high_ref, low_ref):
    for c in range(STEPS):
        w = w_ref[:, cols(c)]
        high = w.astype(BF16)
        high_ref[:, cols(c)] = high
        low_ref[:, cols(c)] = (w - high.astype(F32)).astype(BF16)


def halves(w):
    out = pltpu.VMEM((ROWS, COLS), BF16)
    return kernel(halves_kernel, (out, out), [IN_VMEM], "halves", flops=10**9)(vmem(w))


def left_kernel(ks, *refs):
    n = len(ks)
    q_refs, (g_ref, e_ref, high_ref, low_ref), acc_ref, o_ref = refs[:n], refs[n : n + 4], refs[n + 4 : -1], refs[-1]
    m = matrix(0)
    acc = [acc_ref[0][i] if acc_ref else jnp.zeros((24, ROWS), F32) for i in range(2)]
    for q_ref, k in zip(q_refs, ks):
        for h in range(2):
            s = half(k, h)
            q = three(block_of(q_ref, 0, h))
            for w in (g_ref[m, :, s], e_ref[m, :, s]):
                acc[0] = acc[0] + lax.dot_general(q, w, NT, preferred_element_type=F32)
            for w in (high_ref[:, s], low_ref[:, s]):
                acc[1] = acc[1] + lax.dot_general(q, w, NT, preferred_element_type=F32)
    if len(o_ref.shape) == 3:
        for i in range(2):
            o_ref[i] = acc[i]
    else:
        for i in range(2):
            o_ref[rows(here() ^ i), :] = fold(acc[i])


def left_part(ks, parts, w, acc=(), last=False):
    out = pltpu.VMEM((16, ROWS) if last else (2, 24, ROWS), F32)
    return kernel(functools.partial(left_kernel, ks), out, [IN_VMEM] * (len(parts) + 4 + len(acc)), "left_factor", flops=10**9)(
        *map(vmem, (*parts, *w, *acc)))


def gram_tile(*ps):
    gram = sum(lax.dot_general(p, p, NT, precision=lax.Precision.HIGHEST, preferred_element_type=F32) for p in ps)
    return jnp.concatenate([gram, jnp.zeros((8, 120), F32)], axis=1)


def mean_of(p0, p1, p2, p3):
    return ((p0[...] + p1[...]) + (p2[...] + p3[...])) * (1.0 / SIDE)


def put_tiles(o_ref, k, h, r):
    for i in range(BLOCK // 128):
        t = (h * (BLOCK // 128) + i) * 8
        o_ref[(slice(t, t + 8),) if k is None else (k, slice(t, t + 8))] = r[:, i * 128 : (i + 1) * 128]


def right_kernel(slot, p0, p1, p2, p3, g_ref, e_ref, o_ref):
    m = matrix(slot)
    p = mean_of(p0, p1, p2, p3)
    p = jnp.where(m == 0, p[0:8], p[8:16])
    pieces = three(p)
    gram = gram_tile(p)
    for k in range(SIDE):
        o_ref[k, DEEP : DEEP + 8, :] = gram
        for h in range(2):
            s = slice(k * QUARTER + h * BLOCK, k * QUARTER + (h + 1) * BLOCK)
            r = jnp.dot(pieces, g_ref[m, :, s], preferred_element_type=F32)
            put_tiles(o_ref, k, h, fold(r + jnp.dot(pieces, e_ref[m, :, s], preferred_element_type=F32)))


def right(slot, p_all, g, e):
    return kernel(
        functools.partial(right_kernel, slot), pltpu.VMEM((SIDE, DEEP + 8, 128), F32), [IN_VMEM] * 6,
        "right_own" if slot == 0 else "right_other", flops=10**9,
    )(*map(vmem, p_all), vmem(g), vmem(e))


def right_both_kernel(ks, p0, p1, p2, p3, g_ref, e_ref, high_ref, low_ref, *o_refs):
    m = matrix(0)
    mean = mean_of(p0, p1, p2, p3)
    if len(o_refs) > len(ks):
        o_refs[-1][...] = mean
    mine, theirs = (jnp.where(core == 0, mean[0:8], mean[8:16]) for core in (here(), here() ^ 1))
    gram = gram_tile(mean[0:8], mean[8:16])
    mine, theirs = three(mine), three(theirs)
    for o_ref, k in zip(o_refs, ks):
        o_ref[DEEP : DEEP + 8, :] = gram
        for h in range(2):
            s = half(k, h)
            r = jnp.dot(mine, g_ref[m, :, s], preferred_element_type=F32) + jnp.dot(mine, e_ref[m, :, s], preferred_element_type=F32)
            r = r + jnp.dot(theirs, high_ref[:, s], preferred_element_type=F32)
            put_tiles(o_ref, None, h, fold(r + jnp.dot(theirs, low_ref[:, s], preferred_element_type=F32)))


def right_both(ks, p_all, w, keep):
    out = (pltpu.VMEM((DEEP + 8, 128), F32),) * len(ks) + ((pltpu.VMEM((16, ROWS), F32),) if keep else ())
    return kernel(functools.partial(right_both_kernel, ks), out, [IN_VMEM] * 8, "right_both", flops=10**9)(*map(vmem, (*p_all, *w)))


def pick_kernel(mine_ref, arrived_ref, _, *o_refs):
    for k, o_ref in zip((3, 2, 1, 0), o_refs):
        o_ref[...] = mine_ref[lax.axis_index("x") ^ k] + arrived_ref[lax.axis_index("x") ^ k]


def pick(mine, arrived, later):
    out = (pltpu.VMEM((DEEP + 8, 128), F32),) * SIDE + (pltpu.VMEM(later.shape, later.dtype),)
    return kernel(pick_kernel, out, [IN_VMEM] * 3, "pick", aliases={2: SIDE})(vmem(mine), vmem(arrived), vmem(later))


def add_kernel(a, b, c, d, *o_refs):
    total = (a[...] + b[...]) + (c[...] + d[...])
    o_refs[0][...] = total[0 : o_refs[0].shape[0]]
    if len(o_refs) > 1:
        o_refs[1][...] = total[DEEP : DEEP + 8]


def add(parts, *rows):
    return kernel(add_kernel, tuple(pltpu.VMEM((r, 128), F32) for r in rows), [IN_VMEM] * SIDE, "add")(*map(vmem, parts))


def hat_pieces(lower, p):
    one, two, rest = split3(small_dot(lower, p))
    pieces = jnp.concatenate([one, one, two, two, one, rest, jnp.zeros((80, ROWS), F32)], axis=0)
    return jnp.concatenate([pieces, jnp.zeros((128, 64), F32)], axis=1).T.astype(BF16)


def lower_kernel(gram_ref, *refs):
    lower = inverse_lower(gram_ref[...])
    if len(refs) > 1:
        p_ref, o_ref, hat_ref = refs
        hat_ref[...] = hat_pieces(lower, p_ref[rows(here()), :])
    refs[-2 if len(refs) > 1 else 0][...] = lower


def lower_inverse(gram, p):
    out = (pltpu.VMEM((8, 128), F32),) + ((pltpu.VMEM((256, 128), BF16),) if p else ())
    return kernel(lower_kernel, out, [IN_VMEM] * (1 + len(p)), "lower_inverse", flops=10**9)(vmem(gram), *map(vmem, p))


def normal_kernel(z0, z1, z2, z3, lower_ref, *refs):
    o_ref = refs[-1]
    total = ((z0[...] + z1[...]) + (z2[...] + z3[...])) * (1.0 / SIDE)
    lower = lower_ref[...]
    for t in range(DEEP // 8):
        o_ref[t * 8 : t * 8 + 8, :] = small_dot(lower, total[t * 8 : t * 8 + 8])


def normal(z_all, lower, first):
    return kernel(normal_kernel, pltpu.VMEM((DEEP, 128), F32), [IN_VMEM] * (5 + len(first)), "normal")(*map(vmem, (*z_all, lower, *first)))


def join_kernel(q0, q1, q2, q3, lower_ref, p_ref, o_ref):
    for k, q_ref in enumerate((q0, q1, q2, q3)):
        o_ref[k * DEEP : (k + 1) * DEEP, :] = q_ref[...]
    first = SIDE * DEEP
    o_ref[first : first + 8, :] = lower_ref[...]
    p = p_ref[rows(here() ^ 1), :]
    o_ref[first + 8 : first + 16, :] = p[:, 0:128]
    o_ref[first + 16 : first + 24, :] = jnp.concatenate([p[:, 128:ROWS], jnp.zeros((8, 256 - ROWS), F32)], axis=1)


def join(parts, lower, p):
    return kernel(join_kernel, pltpu.VMEM((SIDE * DEEP + 24, 128), F32), [IN_VMEM] * 6, "join")(*map(vmem, (*parts, lower, p)))


def final_kernel(slot, ks, n_q, n_in, *refs):
    q_refs, hat_ref, (g_ref, e_ref) = refs[:n_q], refs[n_q:n_in], refs[n_in : n_in + 2]
    a_hbm, n_hbm, q_hbm, a_buf, n_buf, q_buf, a_sem, n_sem, q_sem = refs[-9:]
    m = matrix(slot)
    copies = []
    if hat_ref:
        hat = hat_ref[0][...]
    else:
        lower, p = q_refs[0][SIDE * DEEP : SIDE * DEEP + 8, :], q_refs[0][SIDE * DEEP + 8 :, :]
        hat = hat_pieces(lower, jnp.concatenate([p[0:8], p[8:16, 0 : ROWS - 128]], axis=1))
    hat = hat[0:ROWS, 0:48]
    for j, k in enumerate(ks):
        for h in range(2):
            i = j * 2 + h
            s = half(k, h)
            q = block_of(q_refs[j], 0, h) if slot == 0 else block_of(q_refs[0], k, h)
            q_buf[i] = q
            one, two, rest = split3(q)
            pieces = jnp.concatenate([one, two, one, two, rest, one], axis=0).astype(BF16)
            full = jnp.dot(hat, pieces, preferred_element_type=F32)
            a_buf[i] = full.astype(BF16)
            n_buf[i] = (g_ref[m, :, s].astype(F32) + e_ref[m, :, s].astype(F32) - full).astype(BF16)
            copies.append(pltpu.make_async_copy(a_buf.at[i], a_hbm.at[m, :, s], a_sem.at[i]))
            copies.append(pltpu.make_async_copy(n_buf.at[i], n_hbm.at[0, m, :, s], n_sem.at[i]))
            copies.append(pltpu.make_async_copy(q_buf.at[i], q_hbm.at[m, :, s], q_sem.at[i]))
            for copy in copies[-3:]:
                copy.start()
    for copy in copies:
        copy.wait()


def final(slot, ks, parts, hat, g, e, before=()):
    n = len(ks) * 2
    n_in = len(parts) + len(hat)
    return pl.pallas_call(
        functools.partial(final_kernel, slot, ks, len(parts), n_in),
        in_specs=[IN_VMEM] * (n_in + 2) + [ANYWHERE] * len(before),
        out_specs=(ANYWHERE,) * 3,
        out_shape=(jax.ShapeDtypeStruct((MATS, ROWS, COLS), BF16), jax.ShapeDtypeStruct((1, MATS, ROWS, COLS), BF16),
                   jax.ShapeDtypeStruct((MATS, RANK, COLS), F32)),
        scratch_shapes=[pltpu.VMEM((n, ROWS, BLOCK), BF16), pltpu.VMEM((n, ROWS, BLOCK), BF16),
                        pltpu.VMEM((n, RANK, BLOCK), F32)] + [pltpu.SemaphoreType.DMA((n,))] * 3,
        input_output_aliases={n_in + 2 + i: i for i in range(len(before))},
        compiler_params=pltpu.CompilerParams(vmem_limit_bytes=16 * 1024 * 1024),
        cost_estimate=pl.CostEstimate(flops=10**9, bytes_accessed=10**6, transcendentals=0),
        name="residual_own" if slot == 0 else "residual_other",
    )(*map(vmem, (*parts, *hat, g, e)), *before)


def swap(a, axis, k):
    return lax.ppermute(a, axis, [(i, i ^ k) for i in range(lax.axis_size(axis))])


def cross(a, axis, k):
    return lax.ppermute(a, (axis, "core"), [(i * 2 + c, (i ^ k) * 2 + (c ^ (k & 1))) for i in range(SIDE) for c in range(2)])


def everyones(a, axis, move, order=(1, 2, 3)):
    moved = {k: move(a, axis, k) for k in order}
    return (a, moved[1], moved[2], moved[3])


def right_sum(parts, p=(), first=()):
    moved = [cross(parts[k], "x", k) for k in (3, 2, 1)]
    (z,) = add((*moved, parts[0]), DEEP + 8)
    z, gram = add(everyones(z, "y", cross), DEEP, 8)
    z_all = everyones(z, "dp", cross)
    lower, *hat = lower_inverse(gram, p)
    return everyones(normal(z_all, lower, first), "x", cross, (2, 1, 3)), lower, hat


def after(parts, out, *ks):
    *late, out = lax.optimization_barrier(tuple(parts[k] for k in ks) + (out,))
    return tuple(late[ks.index(k)] if k in ks else parts[k] for k in range(SIDE)), out


def per_device(grads, errors, q_init):
    p, g, e = first_left(grads, errors, jnp.swapaxes(q_init, 1, 2))
    p_all = everyones(p, "dp", swap)
    arrived = swap(right(1, p_all, g, e), "core", 1)
    z3, z2, z1, z0, w = pick(right(0, p_all, g, e), arrived, working(g, e))
    w = (g, e) + tuple(halves(swap(w, "core", 1)))
    parts, _, _ = right_sum((z0, z1, z2, z3), first=w[2:])

    acc = left_part((0,), parts[:1], w)
    parts, acc = after(parts, left_part((3,), parts[3:], w, (acc,)), 1)
    acc = left_part((1,), parts[1:2], w, (acc,))
    p_all = everyones(left_part((2,), parts[2:3], w, (acc,), True), "dp", cross)
    z2, z3, p = right_both((2, 3), p_all, w, True)
    z1, z0 = right_both((1, 0), p_all, w, False)
    parts, lower, hat = right_sum((z0, z1, z2, z3), (p,))

    out = final(0, (0,), parts[:1], hat, g, e)
    parts, out = after(parts, final(0, (3,), parts[3:], hat, g, e, out), 1, 2)
    other = swap(join(parts, lower, p), "core", 1)
    out = final(0, (1, 2), parts[1:3], hat, g, e, out)
    approx, errors_next, q_next = final(1, (0, 1, 2, 3), (other,), (), g, e, out)
    return approx, errors_next, jnp.swapaxes(q_next, 1, 2)


def solution(mesh):
    fine = Mesh(mesh.devices.reshape(4, 4, 4, 2), ("dp", "x", "y", "core"))
    fsdp = ("x", "y", "core")
    in_specs = (P("dp", None, fsdp, None), P("dp", None, fsdp, None), P())
    out_specs = (P(None, fsdp, None), P("dp", None, fsdp, None), P())
    return jax.shard_map(per_device, mesh=fine, in_specs=in_specs, out_specs=out_specs, check_vma=False)
```
